256 devices in a mesh: blk: 64 (over y, z, x_lo), vocab: 4 (over x_hi, core).
Axes of the slice: x: 4 (x_hi: 2, x_lo: 2; x = x_hi * 2 + x_lo), y: 4, z: 8, core: 2. Of those that a mesh axis runs over, the one named last changes fastest.
Arguments:
- hidden: bfloat16 [45056, 2304], P('blk'), may hold values from -6 to 6
- table: bfloat16 [131072, 2304], P(('blk', 'vocab')), may hold values from -0.25 to 0.25
- targets: int32 [45056], P('blk'), may hold values from 0 to 131071
- group_start: int32 [64], P('blk'), may hold values from 0 to 129024, as said below
- log_norm: float32 [45056], P('blk')
- loss_grad: float32 [45056], P('blk'), may hold values from 4 to 32
Outputs:
- grad_hidden: bfloat16 [45056, 2304], P(('blk', 'vocab'))
- grad_table: float32 [131072, 2304], P(('blk', 'vocab'))
The draws below stay inside these ranges and needn't reach their ends.
Inputs may be any that keep to these rules, and one draw needn't show every extreme that they name: `group_start`: a permutation of the multiples of 2048 below 131072.
All inputs are finite; a program needn't handle non-finite values.
Results may differ from the reference program's by a relative error of at most 0.014.
Values may be sent and summed in bfloat16 or wider, within the bound.
A program may use at most 128 MiB of HBM per device.

```python
import math
import jax
import jax.numpy as jnp
from jax import lax

D = 2304
VC = 512
ROUNDS = 3
TOK_DEV = 704
TOKENS = 45056
VOCAB = 131072
N_BLK = 64
N_VOCAB = 4


def block_starts(key):
    order = jax.random.permutation(jax.random.fold_in(key, 11), N_BLK).astype(jnp.int32)
    return order * (VC * N_VOCAB)


def draw_group_start(key, part):
    return block_starts(key)


def draw_targets(key, part):
    starts = block_starts(key)
    key = jax.random.fold_in(key, 5)
    key_round, key_offset, key_spread, key_pick = jax.random.split(key, 4)
    width = VC * N_VOCAB
    owner = jnp.arange(TOKENS, dtype=jnp.int32) // TOK_DEV
    back = jax.random.randint(key_round, (TOKENS,), 0, ROUNDS, dtype=jnp.int32)
    met_block = (owner - back) % N_BLK
    offset = jax.random.randint(key_offset, (TOKENS,), 0, width, dtype=jnp.int32)
    met_id = starts[met_block] + offset
    spread_id = jax.random.randint(key_spread, (TOKENS,), 0, VOCAB, dtype=jnp.int32)
    pick = jax.random.randint(key_pick, (TOKENS,), 0, 4, dtype=jnp.int32)
    return jnp.where(pick < 2, met_id, spread_id).astype(jnp.int32)


def draw_log_norm(key, part):
    key = jax.random.fold_in(key, 7)
    spread = jax.random.uniform(key, (TOKENS,), jnp.float32, -0.5, 1.5)
    return math.log(ROUNDS * VC * N_VOCAB) + 2.0 + spread


def level_of(key, extent, cuts, least, top_value):
    gain, own = 1.0, jax.random.fold_in(key, 6)
    for axis_at, blocks in cuts:
        steps = jnp.exp(jax.random.uniform(jax.random.fold_in(own, axis_at), (blocks,), jnp.float32, least / len(cuts), top_value / len(cuts)))
        gain = gain * jnp.repeat(steps, extent[axis_at] // blocks).reshape([-1 if axis == axis_at else 1 for axis in range(len(extent))])
    return gain


def centred(stream_key, dims, deviation, limit, shards=(), held_as=jnp.bfloat16):
    entries = jax.random.normal(stream_key, dims, jnp.float32) * deviation
    if len(shards) > 0:
        entries = level_of(stream_key, dims, shards, -0.22, 0.18) * entries
    return jnp.clip(entries, min=-limit, max=limit).astype(held_as)


def setup_inputs(seed: int = 0) -> dict:
    keys = jax.random.split(jax.random.key(seed), 7)
    hidden = centred(keys[0], (TOKENS, D), 1.0, 6.0, ((0, 64),))
    table = centred(keys[1], (VOCAB, D), (D // 4) ** -0.5, 0.25, ((0, 256),))
    targets = draw_targets(jax.random.fold_in(keys[6], 71), 0)
    group_start = draw_group_start(jax.random.fold_in(keys[6], 71), 0)
    log_norm = draw_log_norm(jax.random.fold_in(keys[6], 71), 0)
    loss_grad = jnp.clip(jnp.exp(math.log(32.0) - 2.0794415 * jax.random.uniform(keys[5], (TOKENS,), jnp.float32) ** level_of(keys[5], (TOKENS,), ((0, 64),), -0.2, 0.2)), 4.0, 32.0)
    return dict(hidden=hidden, table=table, targets=targets, group_start=group_start, log_norm=log_norm, loss_grad=loss_grad)


def reference(hidden, table, targets, group_start, log_norm, loss_grad):
    width = VC * N_VOCAB
    hid = hidden.reshape(N_BLK, TOK_DEV, D)
    tab = table.reshape(N_BLK, width, D)
    tgt = targets.reshape(N_BLK, TOK_DEV)
    lnorm = log_norm.reshape(N_BLK, TOK_DEV)
    lgrad = loss_grad.reshape(N_BLK, TOK_DEV)

    def slope_of(b, c):
        logits = jnp.dot(hid[b], tab[c].T, preferred_element_type=jnp.float32)
        ids = group_start[c] + jnp.arange(width, dtype=jnp.int32)
        hit = (tgt[b][:, None] == ids[None, :]).astype(jnp.float32)
        prob = jnp.exp(logits - lnorm[b][:, None])
        return (lgrad[b][:, None] * (prob - hit)).astype(jnp.bfloat16)

    def hidden_block(b):
        total = jnp.zeros((N_VOCAB, TOK_DEV, D), jnp.float32)
        for r in range(ROUNDS):
            c = (b - r) % N_BLK
            slope = slope_of(b, c).astype(jnp.float32).reshape(TOK_DEV, N_VOCAB, VC)
            rows = tab[c].astype(jnp.float32).reshape(N_VOCAB, VC, D)
            total = total + jnp.einsum("tvk,vkd->vtd", slope, rows)
        partial_value = total.astype(jnp.bfloat16).astype(jnp.float32)
        return jnp.sum(partial_value, axis=0).astype(jnp.bfloat16)

    def table_block(c):
        total = jnp.zeros((width, D), jnp.float32)
        for r in range(ROUNDS):
            b = (c + r) % N_BLK
            total = total + jnp.dot(slope_of(b, c).T, hid[b], preferred_element_type=jnp.float32)
        return total

    index = jnp.arange(N_BLK, dtype=jnp.int32)
    grad_hidden = lax.map(hidden_block, index).reshape(TOKENS, D)
    blocks = lax.map(table_block, index)
    grad_table = jnp.roll(blocks, ROUNDS - 1, axis=0).reshape(VOCAB, D)
    return grad_hidden, grad_table
```

```python
import functools

import jax
import jax.numpy as jnp
from jax import lax
from jax.experimental import pallas as pl
from jax.experimental.pallas import tpu as pltpu
from jax.sharding import PartitionSpec as P

MESH = pl.DeviceIdType.MESH
CHUNKS = 4
GROUP = 256
WIDE = 768
F32, BF16 = jnp.float32, jnp.bfloat16


def remote(src, dst, sems, device):
    return pltpu.make_async_remote_copy(
        src_ref=src, dst_ref=dst, send_sem=sems[0], recv_sem=sems[1],
        device_id=device, device_id_type=MESH,
    )


def kernel(
    rows_of_ring, aux_ref, hid_hbm, tab_hbm, gh_out, gt_out,
    hid, oth, tab, arr, aux_oth, aux_arr, cols,
    s_own, s_oth, s_arr, t_own, t_oth, t_arr,
    grad, dwp, dwr, keep, cc_out, cc_in, x_out, x_in, gh_vmem,
    lsem, osem, bs, br, ts, tr, ps, pr, hs, hr, rs, rr, cs, cr, xs, xr, as_, ar,
):
    tokens, width = hid.shape
    vocab = tab.shape[0]
    quarter = tokens // 4
    blk, part = lax.axis_index("blk"), lax.axis_index("vocab")
    row, lo = blk // 2, blk % 2
    hi, core = part // 2, part % 2

    def at(r, low, high, c):
        return (((r + rows_of_ring) % rows_of_ring) * 2 + low, high * 2 + c)

    up, down = at(row + 1, lo, hi, core), at(row - 1, lo, hi, core)
    across = at(row, lo, 1 - hi, core)
    side = [at(row, 1 - lo, h, core) for h in range(2)]
    sibling = at(row, lo, hi, 1 - core)

    load_hid = pltpu.make_async_copy(hid_hbm, hid, lsem.at[0])
    load_tab = pltpu.make_async_copy(tab_hbm, tab, lsem.at[1])
    load_hid.start()
    load_tab.start()

    barrier = pltpu.get_barrier_semaphore()
    for device in (up, down, across, side[0], side[1], sibling):
        pl.semaphore_signal(barrier, inc=1, device_id=device, device_id_type=MESH)
    pl.semaphore_wait(barrier, 6)

    def quarter_of(h, c):
        return pl.ds(pl.multiple_of((h * 2 + c) * quarter, 16), quarter)

    aux_side = remote(aux_ref, aux_oth, (as_.at[0], ar.at[0]), at(row, 1 - lo, hi, core))
    aux_up = remote(aux_ref, aux_arr, (as_.at[1], ar.at[1]), up)
    aux_side.start()
    aux_up.start()

    piece = vocab // CHUNKS

    def piece_of(i):
        return pl.ds(i * piece, piece)

    table_up = [
        remote(tab_hbm.at[piece_of(i)], arr.at[piece_of(i)], (ts.at[i], tr.at[i]), up)
        for i in range(CHUNKS)
    ]
    grad_up = [
        remote(dwp.at[piece_of(i)], dwr.at[piece_of(i)], (ps.at[i], pr.at[i]), up)
        for i in range(CHUNKS)
    ]
    table_up[0].start()
    table_up[1].start()

    mine = quarter_of(hi, core)
    hidden_out = [
        remote(hid_hbm.at[mine], oth.at[mine], (hs.at[h], hr.at[hi]), side[h]) for h in range(2)
    ]
    hidden_in = [
        remote(oth.at[quarter_of(h, core)], oth.at[quarter_of(h, core)], (hs.at[h], hr.at[h]), side[h])
        for h in range(2)
    ]
    for copy in hidden_out:
        copy.start()

    def spread(ref, slot):
        for i in range(ref.shape[1] // 128):
            block = ref[:, i * 128:(i + 1) * 128]
            square = jnp.concatenate([block] * 16, axis=0)
            height = min(128, tokens - i * 128)
            cols[slot, i * 128:i * 128 + height, :] = square.T[:height]

    def slope(hid_ref, tab_ref, slot, base, out, out_t, start):
        group = pl.ds(start, GROUP)
        logits = lax.dot_general(
            hid_ref[...], tab_ref[group, :], (((1,), (1,)), ((), ())), preferred_element_type=F32
        )
        ids = (lax.broadcasted_iota(jnp.int32, (1, GROUP), 1) + (part * vocab + start)).astype(F32)
        hit = (cols[slot, :, 0:1] == base + ids).astype(F32)
        value = cols[slot, :, 2:3] * (jnp.exp(logits - cols[slot, :, 1:2]) - hit)
        out[:, group] = value.astype(BF16)
        out_t[group, :] = value.T.astype(BF16)

    def each_group(body):
        def step(i, carry):
            body(pl.multiple_of(i * GROUP, GROUP))
            return carry
        lax.fori_loop(0, vocab // GROUP, step, 0)

    def each_wide(body):
        def step(i, carry):
            body(pl.ds(pl.multiple_of(i * WIDE, WIDE), WIDE))
            return carry
        lax.fori_loop(0, width // WIDE, step, 0)

    def table_term(terms, start, out, dtype):
        group = pl.ds(start, GROUP)

        def body(wide):
            total = None
            for st, h in terms:
                term = jnp.dot(st[group, :], h[:, wide], preferred_element_type=F32)
                total = term if total is None else total + term
            out[group, wide] = total.astype(dtype)
        each_wide(body)

    def hidden_term(terms, rows, store):
        def body(wide):
            total = None
            for s, t in terms:
                term = jnp.dot(s[rows, :], t[:, wide], preferred_element_type=F32)
                total = term if total is None else total + term
            store(wide, total)
        each_wide(body)

    def core_copy(tok, h):
        slot = tok * 2 + h
        return remote(cc_out.at[slot], cc_in.at[slot], (cs.at[slot], cr.at[slot]), sibling)

    def halve(tok, terms):
        for h in range(2):
            def put(wide, value, slot=tok * 2 + h):
                cc_out[slot, :, wide] = value.astype(BF16)
            hidden_term(terms, quarter_of(h, 1 - core), put)
            core_copy(tok, h).start()
        for h in range(2):
            def put(wide, value, slot=tok * 2 + h):
                keep[slot, :, wide] = value
            hidden_term(terms, quarter_of(h, core), put)

    def x_copy(slot, dst_slot, device):
        return remote(x_out.at[slot], x_in.at[dst_slot], (xs.at[slot], xr.at[dst_slot]), device)

    def send_other():
        for h in range(2):
            core_copy(1, h).wait_recv()
            x_out[1 + h] = (keep[2 + h] + cc_in[2 + h].astype(F32)).astype(BF16)
            x_copy(1 + h, 1 + hi, side[h]).start()

    spread(aux_ref, 0)
    load_hid.wait()
    load_tab.wait()
    base_own = aux_ref[3:4, 0:1]
    each_group(lambda start: slope(hid, tab, 0, base_own, s_own, t_own, start))

    relay = [
        remote(oth.at[quarter_of(h, core)], oth.at[quarter_of(h, core)], (rs.at[h], rr.at[h]), sibling)
        for h in range(2)
    ]
    table_up[0].wait_send()
    table_up[2].start()
    for h in range(2):
        hidden_in[h].wait_recv()
        relay[h].start()
    aux_side.wait_recv()
    spread(aux_oth, 1)
    for h in range(2):
        relay[h].wait_recv()

    @pl.when(lo == 0)
    def _():
        each_group(lambda start: slope(oth, tab, 1, base_own, s_oth, t_oth, start))
        each_group(lambda start: table_term([(t_own, hid), (t_oth, oth)], start, dwp, BF16))
        halve(1, [(s_oth, tab)])
        send_other()

    @pl.when(lo == 1)
    def _():
        each_group(lambda start: table_term([(t_own, hid)], start, dwp, BF16))

    aux_up.wait_recv()
    base_arr = aux_arr[3:4, 0:1]
    table_up[1].wait_send()
    table_up[3].start()

    def arrived(start):
        slope(hid, arr, 0, base_arr, s_arr, t_arr, start)

        @pl.when(lo == 0)
        def _():
            table_term([(t_arr, hid)], start, grad, F32)

        @pl.when(lo == 1)
        def _():
            slope(oth, arr, 1, base_arr, s_oth, t_oth, start)
            table_term([(t_arr, hid), (t_oth, oth)], start, grad, F32)

    table_up[0].wait_recv()
    table_up[1].wait_recv()
    arrived(0)
    table_up[2].wait_send()
    grad_up[0].start()
    table_up[3].wait_send()
    grad_up[1].start()
    table_up[2].wait_recv()
    table_up[3].wait_recv()
    arrived(GROUP)

    @pl.when(lo == 1)
    def _():
        halve(1, [(s_oth, arr)])
        send_other()

    halve(0, [(s_own, tab), (s_arr, arr)])
    for h in range(2):
        core_copy(0, h).wait_recv()
    x_out[0] = (keep[1 - hi] + cc_in[1 - hi].astype(F32)).astype(BF16)
    x_copy(0, 0, across).start()
    grad_up[0].wait_send()
    grad_up[2].start()
    grad_up[1].wait_send()
    grad_up[3].start()

    outs = [
        pltpu.make_async_copy(grad.at[piece_of(i)], gt_out.at[piece_of(i)], osem.at[i])
        for i in range(CHUNKS)
    ]

    def finish(i):
        grad_up[i].wait_recv()
        grad[piece_of(i)] = grad[piece_of(i)] + dwr[piece_of(i)].astype(F32)
        outs[i].start()

    finish(0)
    finish(1)
    for slot, device in ((0, across), (1, side[0]), (2, side[1])):
        x_copy(slot, slot, device).wait_recv()
    total = keep[hi] + cc_in[hi].astype(F32)
    for slot in range(3):
        total = total + x_in[slot].astype(F32)
    gh_vmem[...] = total.astype(BF16)
    out_gh = pltpu.make_async_copy(gh_vmem, gh_out, osem.at[CHUNKS])
    out_gh.start()
    for i in range(2, CHUNKS):
        finish(i)

    aux_side.wait_send()
    aux_up.wait_send()
    for copy in hidden_out:
        copy.wait_send()
    for copy in relay:
        copy.wait_send()
    for tok in range(2):
        for h in range(2):
            core_copy(tok, h).wait_send()
    for slot, device in ((0, across), (1, side[0]), (2, side[1])):
        x_copy(slot, slot, device).wait_send()
    grad_up[2].wait_send()
    grad_up[3].wait_send()
    out_gh.wait()
    for copy in outs:
        copy.wait()


def per_device(rows_of_ring, hidden, table, targets, group_start, log_norm, loss_grad):
    tokens, width = hidden.shape
    vocab = table.shape[0]
    quarter = tokens // 4
    padded = -(-tokens // 128) * 128
    aux = jnp.stack([
        targets.astype(F32), log_norm, loss_grad,
        jnp.broadcast_to(group_start.astype(F32), (tokens,)),
    ])
    aux = jnp.pad(aux, ((0, 4), (0, padded - tokens)))
    dma = pltpu.SemaphoreType.DMA
    return pl.pallas_call(
        functools.partial(kernel, rows_of_ring),
        out_shape=(
            jax.ShapeDtypeStruct((quarter, width), BF16),
            jax.ShapeDtypeStruct((vocab, width), F32),
        ),
        in_specs=[
            pl.BlockSpec(memory_space=pltpu.VMEM),
            pl.BlockSpec(memory_space=pl.ANY),
            pl.BlockSpec(memory_space=pl.ANY),
        ],
        out_specs=[pl.BlockSpec(memory_space=pl.ANY)] * 2,
        scratch_shapes=[
            pltpu.VMEM((tokens, width), BF16),
            pltpu.VMEM((tokens, width), BF16),
            pltpu.VMEM((vocab, width), BF16),
            pltpu.VMEM((vocab, width), BF16),
            pltpu.VMEM((8, padded), F32),
            pltpu.VMEM((8, padded), F32),
            pltpu.VMEM((2, tokens, 128), F32),
            pltpu.VMEM((tokens, vocab), BF16),
            pltpu.VMEM((tokens, vocab), BF16),
            pltpu.VMEM((tokens, vocab), BF16),
            pltpu.VMEM((vocab, tokens), BF16),
            pltpu.VMEM((vocab, tokens), BF16),
            pltpu.VMEM((vocab, tokens), BF16),
            pltpu.VMEM((vocab, width), F32),
            pltpu.VMEM((vocab, width), BF16),
            pltpu.VMEM((vocab, width), BF16),
            pltpu.VMEM((4, quarter, width), F32),
            pltpu.VMEM((4, quarter, width), BF16),
            pltpu.VMEM((4, quarter, width), BF16),
            pltpu.VMEM((3, quarter, width), BF16),
            pltpu.VMEM((3, quarter, width), BF16),
            pltpu.VMEM((quarter, width), BF16),
            dma((2,)), dma((CHUNKS + 1,)),
            dma((1,)), dma((1,)),
            dma((CHUNKS,)), dma((CHUNKS,)),
            dma((CHUNKS,)), dma((CHUNKS,)),
            dma((2,)), dma((2,)),
            dma((2,)), dma((2,)),
            dma((4,)), dma((4,)),
            dma((3,)), dma((3,)),
            dma((2,)), dma((2,)),
        ],
        compiler_params=pltpu.CompilerParams(
            collective_id=1, has_side_effects=True, vmem_limit_bytes=60 * 2**20
        ),
        cost_estimate=pl.CostEstimate(
            flops=18 * tokens * vocab * width, bytes_accessed=12 * tokens * width, transcendentals=3 * tokens * vocab
        ),
    )(aux, hidden, table)


def solution(mesh):
    placed = (P("blk", None), P(("blk", "vocab"), None), P("blk"), P("blk"), P("blk"), P("blk"))
    return jax.shard_map(
        functools.partial(per_device, mesh.shape["blk"] // 2),
        mesh=mesh,
        in_specs=placed,
        out_specs=(P(("blk", "vocab"), None), P(("blk", "vocab"), None)),
        check_vma=False,
    )
```

```python
import functools

import jax
import jax.numpy as jnp
from jax import lax
from jax.experimental import pallas as pl
from jax.experimental.pallas import tpu as pltpu
from jax.sharding import PartitionSpec as P

MESH = pl.DeviceIdType.MESH
GROUP = 256
WIDE = 768
RING, LEG = 8, 3
TABLE_CUTS = tuple((64 * i, 64) for i in range(8))
GRAD_CUTS = tuple((64 * i, 64) for i in range(6)) + ((384, 48),)
LONG_FROM = 432
LONG_CUTS = ((432, 48), (480, 32))
F32, BF16 = jnp.float32, jnp.bfloat16

AUX, SIDE_HID, SIDE_RELAY, CORE, ACROSS = 0, 2, 4, 6, 10
TABLE = 13
GRAD = TABLE + len(TABLE_CUTS)
LONG = GRAD + len(GRAD_CUTS)
COPIES = LONG + 6


def kernel(
    rows_of_ring, tgt_ref, first_ref, norm_ref, cot_ref, hid_hbm, tab_hbm, gh_out, grad,
    hid, oth, tab, arr, aux_ref, aux_oth, aux_arr, cols,
    s_own, s_oth, s_arr, t_own, t_oth, t_arr,
    dwp, dwr, keep, give, cc_out, cc_in, x_out, x_in, way_a, way_b, lsem, send, recv,
):
    tokens, width = hid.shape
    vocab = tab.shape[0]
    quarter = tokens // 4
    blk, part = lax.axis_index("blk"), lax.axis_index("vocab")
    row, lo = blk // 2, blk % 2
    hi, core = part // 2, part % 2
    plane, height = row // RING, row % RING

    def at(r, low, high, c):
        return (((r + rows_of_ring) % rows_of_ring) * 2 + low, high * 2 + c)

    def along(y, z):
        return y * RING + (z + RING) % RING

    up, down = at(row + 1, lo, hi, core), at(row - 1, lo, hi, core)
    across = at(row, lo, 1 - hi, core)
    side = [at(row, 1 - lo, h, core) for h in range(2)]
    sibling = at(row, lo, hi, 1 - core)
    turn_to = lax.rem(height + RING + LEG, RING) == RING - 1
    turn_from = lax.rem(height + 2 * LEG, RING) == RING - 1
    leg_to = at(along(plane, height - LEG), lo, hi, core)
    leg_from = at(along(plane, height + LEG), lo, hi, core)
    turn_to = at(along(plane + turn_to.astype(jnp.int32), height - LEG), lo, hi, core)
    turn_from = at(along(plane - turn_from.astype(jnp.int32), height + LEG), lo, hi, core)
    last_to = at(along(plane, height - 1), lo, hi, core)
    last_from = at(along(plane, height + 1), lo, hi, core)

    load_hid = pltpu.make_async_copy(hid_hbm, hid, lsem.at[0])
    load_tab = pltpu.make_async_copy(tab_hbm, tab, lsem.at[1])
    load_hid.start()
    load_tab.start()

    aux_ref[...] = jnp.zeros_like(aux_ref)
    aux_ref[0:1, :tokens] = tgt_ref[...].astype(F32).reshape(1, tokens)
    aux_ref[1:2, :tokens] = norm_ref[...].reshape(1, tokens)
    aux_ref[2:3, :tokens] = cot_ref[...].reshape(1, tokens)
    aux_ref[3:4, :] = jnp.full((1, aux_ref.shape[1]), first_ref[0].astype(F32), F32)

    barrier = pltpu.get_barrier_semaphore()
    partners = (up, down, across, side[0], side[1], sibling, leg_to, leg_from, turn_to, turn_from, last_to, last_from)
    for device in partners:
        pl.semaphore_signal(barrier, inc=1, device_id=device, device_id_type=MESH)
    pl.semaphore_wait(barrier, len(partners))

    def quarter_of(h, c):
        return pl.ds(pl.multiple_of((h * 2 + c) * quarter, 16), quarter)

    def rows_of(cut):
        return pl.ds(cut[0], cut[1])

    def copy(src, dst, number, device, number_there=None):
        there = number if number_there is None else number_there
        return pltpu.make_async_remote_copy(
            src_ref=src, dst_ref=dst, send_sem=send.at[number], recv_sem=recv.at[there],
            device_id=device, device_id_type=MESH,
        )

    table_up = [copy(tab_hbm.at[rows_of(c)], arr.at[rows_of(c)], TABLE + i, up) for i, c in enumerate(TABLE_CUTS)]
    grad_up = [copy(dwp.at[rows_of(c)], dwr.at[rows_of(c)], GRAD + i, up) for i, c in enumerate(GRAD_CUTS)]

    def inside(cut):
        return pl.ds(cut[0] - LONG_FROM, cut[1])

    leg_1 = [copy(dwp.at[rows_of(c)], way_a.at[inside(c)], LONG + i, leg_to) for i, c in enumerate(LONG_CUTS)]
    leg_2 = [copy(way_a.at[inside(c)], way_b.at[inside(c)], LONG + 2 + i, turn_to) for i, c in enumerate(LONG_CUTS)]
    leg_3 = [copy(way_b.at[inside(c)], dwr.at[rows_of(c)], LONG + 4 + i, last_to) for i, c in enumerate(LONG_CUTS)]

    mine = quarter_of(hi, core)
    hidden_out = [copy(hid_hbm.at[mine], oth.at[mine], SIDE_HID + h, side[h], SIDE_HID + hi) for h in range(2)]
    hidden_in = [copy(oth.at[quarter_of(h, core)], oth.at[quarter_of(h, core)], SIDE_HID + h, side[h]) for h in range(2)]
    relay = [copy(oth.at[quarter_of(h, core)], oth.at[quarter_of(h, core)], SIDE_RELAY + h, sibling) for h in range(2)]
    aux_side = copy(aux_ref, aux_oth, AUX, at(row, 1 - lo, hi, core))
    aux_up = copy(aux_ref, aux_arr, AUX + 1, up)

    aux_side.start()
    for c in hidden_out:
        c.start()
    aux_up.start()
    for i in range(3):
        table_up[i].start()

    def spread(ref, slot):
        for i in range(ref.shape[1] // 128):
            block = ref[:, i * 128:(i + 1) * 128]
            square = jnp.concatenate([block] * 16, axis=0)
            rest = min(128, tokens - i * 128)
            cols[slot, i * 128:i * 128 + rest, :] = square.T[:rest]

    def slope(hid_ref, tab_ref, slot, base, out, out_t, start):
        group = pl.ds(start, GROUP)
        logits = lax.dot_general(
            hid_ref[...], tab_ref[group, :], (((1,), (1,)), ((), ())), preferred_element_type=F32
        )
        ids = (lax.broadcasted_iota(jnp.int32, (1, GROUP), 1) + (part * vocab + start)).astype(F32)
        hit = (cols[slot, :, 0:1] == base + ids).astype(F32)
        value = cols[slot, :, 2:3] * (jnp.exp(logits - cols[slot, :, 1:2]) - hit)
        out[:, group] = value.astype(BF16)
        out_t[group, :] = value.T.astype(BF16)

    def each_group(body):
        def step(i, carry):
            body(pl.multiple_of(i * GROUP, GROUP))
            return carry
        lax.fori_loop(0, vocab // GROUP, step, 0)

    def each_wide(body):
        def step(i, carry):
            body(pl.ds(pl.multiple_of(i * WIDE, WIDE), WIDE))
            return carry
        lax.fori_loop(0, width // WIDE, step, 0)

    def table_term(terms, start, out, dtype):
        group = pl.ds(start, GROUP)

        def body(wide):
            total = None
            for st, h in terms:
                term = jnp.dot(st[group, :], h[:, wide], preferred_element_type=F32)
                total = term if total is None else total + term
            out[group, wide] = total.astype(dtype)
        each_wide(body)

    def hidden_term(terms, rows, store):
        def body(wide):
            total = None
            for s, t, span in terms:
                term = jnp.dot(s[rows, span], t[span, wide], preferred_element_type=F32)
                total = term if total is None else total + term
            store(wide, total)
        each_wide(body)

    def core_copy(tok, h):
        slot = tok * 2 + h
        return copy(cc_out.at[slot], cc_in.at[slot], CORE + slot, sibling)

    def begin(tok, terms):
        for h in range(2):
            for c, place in ((1 - core, give), (core, keep)):
                def put(wide, value, place=place, slot=tok * 2 + h):
                    place[slot, :, wide] = value
                hidden_term(terms, quarter_of(h, c), put)

    def halve(tok, terms, begun):
        for h in range(2):
            def put(wide, value, slot=tok * 2 + h):
                if begun:
                    value = value + give[slot, :, wide]
                cc_out[slot, :, wide] = value.astype(BF16)
            hidden_term(terms, quarter_of(h, 1 - core), put)
            core_copy(tok, h).start()
        for h in range(2):
            def put(wide, value, slot=tok * 2 + h):
                if begun:
                    value = value + keep[slot, :, wide]
                keep[slot, :, wide] = value
            hidden_term(terms, quarter_of(h, core), put)

    def x_copy(slot, dst_slot, device):
        return copy(x_out.at[slot], x_in.at[dst_slot], ACROSS + slot, device, ACROSS + dst_slot)

    def send_other():
        for h in range(2):
            core_copy(1, h).wait_recv()
            x_out[1 + h] = (keep[2 + h] + cc_in[2 + h].astype(F32)).astype(BF16)
            x_copy(1 + h, 1 + hi, side[h]).start()

    whole, first, second = pl.ds(0, vocab), pl.ds(0, GROUP), pl.ds(GROUP, GROUP)

    spread(aux_ref, 0)
    load_hid.wait()
    load_tab.wait()
    base_own = aux_ref[3:4, 0:1]
    each_group(lambda start: slope(hid, tab, 0, base_own, s_own, t_own, start))

    table_up[0].wait_send()
    table_up[3].start()
    for h in range(2):
        hidden_in[h].wait_recv()
        relay[h].start()
    aux_side.wait_recv()
    spread(aux_oth, 1)
    for h in range(2):
        relay[h].wait_recv()
    for i in range(1, 3):
        table_up[i].wait_send()
        table_up[i + 3].start()

    @pl.when(lo == 0)
    def _():
        each_group(lambda start: slope(oth, tab, 1, base_own, s_oth, t_oth, start))
        table_term([(t_own, hid), (t_oth, oth)], GROUP, dwp, BF16)
        for c in leg_1:
            c.start()
        halve(1, [(s_oth, tab, whole)], False)
        send_other()
        table_term([(t_own, hid), (t_oth, oth)], 0, dwp, BF16)

    @pl.when(lo == 1)
    def _():
        table_term([(t_own, hid)], GROUP, dwp, BF16)
        for c in leg_1:
            c.start()
        table_term([(t_own, hid)], 0, dwp, BF16)

    for i in range(3, 5):
        table_up[i].wait_send()
        table_up[i + 3].start()

    aux_up.wait_recv()
    base_arr = aux_arr[3:4, 0:1]
    for i in range(4):
        table_up[i].wait_recv()
    slope(hid, arr, 0, base_arr, s_arr, t_arr, 0)

    @pl.when(lo == 0)
    def _():
        begin(0, [(s_own, tab, whole), (s_arr, arr, first)])
        table_term([(t_arr, hid)], 0, grad, F32)

    @pl.when(lo == 1)
    def _():
        slope(oth, arr, 1, base_arr, s_oth, t_oth, 0)
        begin(1, [(s_oth, arr, first)])
        begin(0, [(s_own, tab, whole), (s_arr, arr, first)])
        table_term([(t_arr, hid), (t_oth, oth)], 0, grad, F32)

    leg_1[0].wait_recv()
    leg_2[0].start()
    for i in range(5, 8):
        table_up[i].wait_send()
    for i in range(3):
        grad_up[i].start()

    for i in range(4, 8):
        table_up[i].wait_recv()

    @pl.when(lo == 1)
    def _():
        slope(oth, arr, 1, base_arr, s_oth, t_oth, GROUP)
        halve(1, [(s_oth, arr, second)], True)

    leg_1[1].wait_recv()
    leg_2[1].start()
    slope(hid, arr, 0, base_arr, s_arr, t_arr, GROUP)

    @pl.when(lo == 1)
    def _():
        send_other()

    halve(0, [(s_arr, arr, second)], True)
    for h in range(2):
        core_copy(0, h).wait_recv()
    x_out[0] = (keep[1 - hi] + cc_in[1 - hi].astype(F32)).astype(BF16)
    x_copy(0, 0, across).start()
    grad_up[0].wait_send()
    grad_up[3].start()

    @pl.when(lo == 0)
    def _():
        table_term([(t_arr, hid)], GROUP, grad, F32)

    @pl.when(lo == 1)
    def _():
        table_term([(t_arr, hid), (t_oth, oth)], GROUP, grad, F32)

    def finish(cut):
        grad[rows_of(cut)] = grad[rows_of(cut)] + dwr[rows_of(cut)].astype(F32)

    count = len(GRAD_CUTS)
    leg_2[0].wait_recv()
    leg_3[0].start()
    for i in range(count):
        if i + 4 < count:
            grad_up[i + 1].wait_send()
            grad_up[i + 4].start()
        if i == 2:
            leg_2[1].wait_recv()
            leg_3[1].start()
        if i < count - 1:
            grad_up[i].wait_recv()
            finish(GRAD_CUTS[i])
    for i in range(2):
        leg_3[i].wait_recv()
        finish(LONG_CUTS[i])
    for slot, device in ((0, across), (1, side[0]), (2, side[1])):
        x_copy(slot, slot, device).wait_recv()
    total = keep[hi] + cc_in[hi].astype(F32)
    for slot in range(3):
        total = total + x_in[slot].astype(F32)
    gh_out[...] = total.astype(BF16)
    grad_up[count - 1].wait_recv()
    finish(GRAD_CUTS[count - 1])

    aux_side.wait_send()
    aux_up.wait_send()
    for c in hidden_out + relay + leg_1 + leg_2 + leg_3 + grad_up[count - 3:]:
        c.wait_send()
    for tok in range(2):
        for h in range(2):
            core_copy(tok, h).wait_send()
    for slot, device in ((0, across), (1, side[0]), (2, side[1])):
        x_copy(slot, slot, device).wait_send()


def per_device(rows_of_ring, hidden, table, targets, group_start, log_norm, loss_grad):
    tokens, width = hidden.shape
    vocab = table.shape[0]
    quarter = tokens // 4
    padded = -(-tokens // 128) * 128
    dma = pltpu.SemaphoreType.DMA
    return pl.pallas_call(
        functools.partial(kernel, rows_of_ring),
        out_shape=(
            pltpu.VMEM((quarter, width), BF16),
            pltpu.VMEM((vocab, width), F32),
        ),
        in_specs=[
            pl.BlockSpec(memory_space=pltpu.VMEM),
            pl.BlockSpec(memory_space=pltpu.SMEM),
            pl.BlockSpec(memory_space=pltpu.VMEM),
            pl.BlockSpec(memory_space=pltpu.VMEM),
            pl.BlockSpec(memory_space=pl.ANY),
            pl.BlockSpec(memory_space=pl.ANY),
        ],
        out_specs=[pl.BlockSpec(memory_space=pltpu.VMEM)] * 2,
        scratch_shapes=[
            *[pltpu.VMEM((tokens, width), BF16)] * 2,
            *[pltpu.VMEM((vocab, width), BF16)] * 2,
            *[pltpu.VMEM((8, padded), F32)] * 3,
            pltpu.VMEM((2, tokens, 128), F32),
            *[pltpu.VMEM((tokens, vocab), BF16)] * 3,
            *[pltpu.VMEM((vocab, tokens), BF16)] * 3,
            *[pltpu.VMEM((vocab, width), BF16)] * 2,
            *[pltpu.VMEM((4, quarter, width), F32)] * 2,
            *[pltpu.VMEM((4, quarter, width), BF16)] * 2,
            *[pltpu.VMEM((3, quarter, width), BF16)] * 2,
            *[pltpu.VMEM((vocab - LONG_FROM, width), BF16)] * 2,
            dma((2,)), dma((COPIES,)), dma((COPIES,)),
        ],
        compiler_params=pltpu.CompilerParams(
            collective_id=1, has_side_effects=True, vmem_limit_bytes=56 * 2**20
        ),
        cost_estimate=pl.CostEstimate(
            flops=18 * tokens * vocab * width, bytes_accessed=12 * tokens * width, transcendentals=3 * tokens * vocab
        ),
    )(targets, group_start, log_norm, loss_grad, hidden, table)


def solution(mesh):
    placed = (P("blk", None), P(("blk", "vocab"), None), P("blk"), P("blk"), P("blk"), P("blk"))
    return jax.shard_map(
        functools.partial(per_device, mesh.shape["blk"] // 2),
        mesh=mesh,
        in_specs=placed,
        out_specs=(P(("blk", "vocab"), None), P(("blk", "vocab"), None)),
        check_vma=False,
    )
```

```python
import functools

import jax
import jax.numpy as jnp
from jax import lax
from jax.experimental import pallas as pl
from jax.experimental.pallas import tpu as pltpu
from jax.sharding import PartitionSpec as P

MESH = pl.DeviceIdType.MESH
GROUP = 256
WIDE = 768
RING, LEG = 8, 3
TABLE_CUTS = tuple((64 * i, 64) for i in range(8))
GRAD_CUTS = tuple((64 * i, 64) for i in range(5)) + ((320, 16),)
SIDE_CUTS = ((336, 48), (384, 48))
LONG_CUTS = ((432, 48), (480, 32))
SIDE_PARTS = ((0, 0, 32), (1, 0, 32), (0, 32, 16), (1, 32, 16))
LONG_ROWS = 112
HID_CUTS = ((0, 0, 64), (0, 64, 64), (0, 128, 48), (1, 0, 64))
HID_LONG = ((1, 64, 64), (1, 128, 48))
HID_SHARE = ((0, 0, 176), (1, 0, 64)) + HID_LONG
F32, BF16 = jnp.float32, jnp.bfloat16

AUX, SIDE_HID, SIDE_RELAY, CORE, CROSS, SIDE = 0, 2, 4, 6, 10, 12
TABLE = 16
GRAD = TABLE + len(TABLE_CUTS)
LONG = GRAD + len(GRAD_CUTS)
HID_UP = LONG + 6
HID_RELAY = HID_UP + len(HID_CUTS)
BY_SIDE = HID_RELAY + len(HID_SHARE)
BY_UP = BY_SIDE + 2
BY_BACK = BY_UP + 4
COPIES = BY_BACK + 4


def kernel(
    rows_of_ring, tgt_ref, first_ref, norm_ref, cot_ref, hid_hbm, tab_hbm, gh_out, grad,
    hid, oth, thr, tab, arr, aux_ref, aux_oth, aux_arr, cols,
    s_own, s_oth, s_arr, t_own, t_oth, t_arr, t_thr,
    dwp, dwr, keep, give, cc_out, cc_in, x_out, x_in, m_in, way_a, way_b, by_in, by_up, lsem, send, recv,
):
    tokens, width = hid.shape
    vocab = tab.shape[0]
    quarter = tokens // 4
    blk, part = lax.axis_index("blk"), lax.axis_index("vocab")
    row, lo = blk // 2, blk % 2
    hi, core = part // 2, part % 2
    plane, height = row // RING, row % RING

    def at(r, low, high, c):
        return (((r + rows_of_ring) % rows_of_ring) * 2 + low, high * 2 + c)

    def along(y, z):
        return y * RING + (z + RING) % RING

    up, down = at(row + 1, lo, hi, core), at(row - 1, lo, hi, core)
    side = [at(row, 1 - lo, h, core) for h in range(2)]
    sibling = at(row, lo, hi, 1 - core)
    turn_to = lax.rem(height + RING + LEG, RING) == RING - 1
    turn_from = lax.rem(height + 2 * LEG, RING) == RING - 1
    leg_to = at(along(plane, height - LEG), lo, hi, core)
    leg_from = at(along(plane, height + LEG), lo, hi, core)
    turn_to = at(along(plane + turn_to.astype(jnp.int32), height - LEG), lo, hi, core)
    turn_from = at(along(plane - turn_from.astype(jnp.int32), height + LEG), lo, hi, core)
    last_to = at(along(plane, height - 1), lo, hi, core)
    last_from = at(along(plane, height + 1), lo, hi, core)

    barrier = pltpu.get_barrier_semaphore()
    partners = (up, down, side[0], side[1], sibling, leg_to, leg_from, turn_to, turn_from, last_to, last_from)
    for device in partners:
        pl.semaphore_signal(barrier, inc=1, device_id=device, device_id_type=MESH)

    load_hid = pltpu.make_async_copy(hid_hbm, hid, lsem.at[0])
    load_tab = pltpu.make_async_copy(tab_hbm, tab, lsem.at[1])
    load_hid.start()
    load_tab.start()

    aux_ref[...] = jnp.zeros_like(aux_ref)
    aux_ref[0:1, :tokens] = tgt_ref[...].astype(F32).reshape(1, tokens)
    aux_ref[1:2, :tokens] = norm_ref[...].reshape(1, tokens)
    aux_ref[2:3, :tokens] = cot_ref[...].reshape(1, tokens)
    aux_ref[3:4, :] = jnp.full((1, aux_ref.shape[1]), first_ref[0].astype(F32), F32)

    pl.semaphore_wait(barrier, len(partners))

    def quarter_of(h, c):
        return pl.ds(pl.multiple_of((h * 2 + c) * quarter, 16), quarter)

    def rows_of(cut):
        return pl.ds(cut[0], cut[1])

    def copy(src, dst, number, device, number_there=None):
        there = number if number_there is None else number_there
        return pltpu.make_async_remote_copy(
            src_ref=src, dst_ref=dst, send_sem=send.at[number], recv_sem=recv.at[there],
            device_id=device, device_id_type=MESH,
        )

    table_up = [copy(tab_hbm.at[rows_of(c)], arr.at[rows_of(c)], TABLE + i, up) for i, c in enumerate(TABLE_CUTS)]
    grad_up = [copy(dwp.at[rows_of(c)], dwr.at[rows_of(c)], GRAD + i, up) for i, c in enumerate(GRAD_CUTS)]

    def piece_of(cut):
        return pl.ds(pl.multiple_of((cut[0] * 2 + core) * quarter + cut[1], 16), cut[2])

    def legs(sources, targets, sizes):
        first, second, third, place = [], [], [], 0
        for i, (source, target, size) in enumerate(zip(sources, targets, sizes)):
            stop = pl.ds(place, size)
            first.append(copy(source, way_a.at[stop], LONG + i, leg_to))
            second.append(copy(way_a.at[stop], way_b.at[stop], LONG + 2 + i, turn_to))
            third.append(copy(way_b.at[stop], target, LONG + 4 + i, last_to))
            place += size
        return first, second, third

    leg_1, leg_2, leg_3 = legs(
        [dwp.at[rows_of(c)] for c in LONG_CUTS], [dwr.at[rows_of(c)] for c in LONG_CUTS], [c[1] for c in LONG_CUTS]
    )
    leg_1_odd, leg_2_odd, leg_3_odd = legs(
        [hid_hbm.at[piece_of(h)] for h in HID_LONG], [thr.at[piece_of(h)] for h in HID_LONG], [h[2] for h in HID_LONG]
    )

    hid_up = [copy(hid_hbm.at[piece_of(h)], thr.at[piece_of(h)], HID_UP + i, up) for i, h in enumerate(HID_CUTS)]
    hid_relay = [copy(thr.at[piece_of(h)], thr.at[piece_of(h)], HID_RELAY + i, sibling) for i, h in enumerate(HID_SHARE)]

    by_side = [copy(dwp.at[rows_of(c)], by_in.at[hi], BY_SIDE + g, side[g], BY_SIDE + hi) for g, c in enumerate(SIDE_CUTS)]
    by_side_in = [copy(by_in.at[h], by_in.at[h], BY_SIDE + h, side[h]) for h in range(2)]
    by_above, by_back, by_back_in = [], [], []
    for j, (h, low, size) in enumerate(SIDE_PARTS):
        there = SIDE_CUTS[0][0] + low
        rows = pl.ds(low, size)
        back = pl.ds(pl.multiple_of(there + hi * SIDE_CUTS[0][1], 16), size)
        by_above.append(copy(by_in.at[h, rows], by_up.at[h, rows], BY_UP + j, up))
        by_back.append(copy(by_up.at[h, rows], dwr.at[back], BY_BACK + j, side[h], BY_BACK + 2 * (j // 2) + hi))
        landed = pl.ds(there + h * SIDE_CUTS[0][1], size)
        by_back_in.append(copy(by_up.at[h, rows], dwr.at[landed], BY_BACK + j, side[h]))

    mine = quarter_of(hi, core)
    hidden_out = [copy(hid_hbm.at[mine], oth.at[mine], SIDE_HID + h, side[h], SIDE_HID + hi) for h in range(2)]
    hidden_in = [copy(oth.at[quarter_of(h, core)], oth.at[quarter_of(h, core)], SIDE_HID + h, side[h]) for h in range(2)]
    relay = [copy(oth.at[quarter_of(h, core)], oth.at[quarter_of(h, core)], SIDE_RELAY + h, sibling) for h in range(2)]
    aux_side = copy(aux_ref, aux_oth, AUX, at(row, 1 - lo, hi, core))
    aux_up = copy(aux_ref, aux_arr, AUX + 1, up)

    aux_side.start()
    for c in hidden_out:
        c.start()
    aux_up.start()
    for i in range(3):
        table_up[i].start()

    @pl.when(lo == 1)
    def _():
        for c in leg_1_odd:
            c.start()

    def spread(ref, slot):
        for i in range(ref.shape[1] // 128):
            block = ref[:, i * 128:(i + 1) * 128]
            square = jnp.concatenate([block] * 16, axis=0)
            rest = min(128, tokens - i * 128)
            cols[slot, i * 128:i * 128 + rest, :] = square.T[:rest]

    def slope(hid_ref, tab_ref, slot, base, out, out_t, start):
        group = pl.ds(start, GROUP)
        logits = lax.dot_general(
            hid_ref[...], tab_ref[group, :], (((1,), (1,)), ((), ())), preferred_element_type=F32
        )
        ids = (lax.broadcasted_iota(jnp.int32, (1, GROUP), 1) + (part * vocab + start)).astype(F32)
        hit = (cols[slot, :, 0:1] == base + ids).astype(F32)
        value = cols[slot, :, 2:3] * (jnp.exp(logits - cols[slot, :, 1:2]) - hit)
        if out is not None:
            out[:, group] = value.astype(BF16)
        out_t[group, :] = value.T.astype(BF16)

    def each_group(body):
        def step(i, carry):
            body(pl.multiple_of(i * GROUP, GROUP))
            return carry
        lax.fori_loop(0, vocab // GROUP, step, 0)

    def each_wide(body):
        def step(i, carry):
            body(pl.ds(pl.multiple_of(i * WIDE, WIDE), WIDE))
            return carry
        lax.fori_loop(0, width // WIDE, step, 0)

    def table_term(terms, start, out, dtype, more=False):
        group = pl.ds(start, GROUP)

        def body(wide):
            total = out[group, wide] if more else None
            for st, h in terms:
                term = jnp.dot(st[group, :], h[:, wide], preferred_element_type=F32)
                total = term if total is None else total + term
            out[group, wide] = total.astype(dtype)
        each_wide(body)

    def hidden_term(terms, rows, store):
        def body(wide):
            total = None
            for s, t, span in terms:
                term = jnp.dot(s[rows, span], t[span, wide], preferred_element_type=F32)
                total = term if total is None else total + term
            store(wide, total)
        each_wide(body)

    def core_copy(tok, h):
        slot = tok * 2 + h
        return copy(cc_out.at[slot], cc_in.at[slot], CORE + slot, sibling)

    def begin(tok, terms):
        for h in range(2):
            for c, place in ((1 - core, give), (core, keep)):
                def put(wide, value, place=place, slot=tok * 2 + h):
                    place[slot, :, wide] = value
                hidden_term(terms, quarter_of(h, c), put)

    def halve(tok, terms, begun):
        for h in range(2):
            def put(wide, value, slot=tok * 2 + h):
                if begun:
                    value = value + give[slot, :, wide]
                cc_out[slot, :, wide] = value.astype(BF16)
            hidden_term(terms, quarter_of(h, 1 - core), put)
            core_copy(tok, h).start()
        for h in range(2):
            def put(wide, value, slot=tok * 2 + h):
                if begun:
                    value = value + keep[slot, :, wide]
                keep[slot, :, wide] = value
            hidden_term(terms, quarter_of(h, core), put)

    half = width // 2

    def columns(g):
        return pl.ds(pl.multiple_of(g * half, 128), half)

    def cross_copy(g):
        return copy(x_out.at[0, :, columns(g)], m_in.at[hi], CROSS + g, side[g], CROSS + hi)

    def cross_arrival(g):
        return copy(x_out.at[0, :, columns(g)], m_in.at[g], CROSS + g, side[g])

    def side_copy(h, late):
        span = columns(hi if late else 1 - hi)
        return copy(
            x_out.at[1 + h, :, span], x_in.at[hi, :, span], SIDE + 2 * h + late, side[h], SIDE + 2 * hi + late
        )

    def side_arrival(h, late):
        span = columns(h if late else 1 - h)
        return copy(x_out.at[1 + h, :, span], x_in.at[h, :, span], SIDE + 2 * h + late, side[h])

    def send_own():
        for h in range(2):
            core_copy(0, h).wait_recv()
        x_out[0] = (keep[1 - hi] + cc_in[1 - hi].astype(F32)).astype(BF16)
        for g in range(2):
            cross_copy(g).start()

    def send_other():
        for h in range(2):
            core_copy(1, h).wait_recv()
            span = columns(1 - hi)
            x_out[1 + h, :, span] = (keep[2 + h, :, span] + cc_in[2 + h, :, span].astype(F32)).astype(BF16)
            side_copy(h, 0).start()

    def send_rest():
        for h in range(2):
            cross_arrival(1 - h).wait_recv()
            span = columns(hi)
            value = keep[2 + h, :, span] + cc_in[2 + h, :, span].astype(F32) + m_in[1 - h].astype(F32)
            x_out[1 + h, :, span] = value.astype(BF16)
            side_copy(h, 1).start()

    whole, first, second = pl.ds(0, vocab), pl.ds(0, GROUP), pl.ds(GROUP, GROUP)

    spread(aux_ref, 0)
    load_hid.wait()
    load_tab.wait()
    base_own = aux_ref[3:4, 0:1]
    each_group(lambda start: slope(hid, tab, 0, base_own, s_own, t_own, start))

    table_up[0].wait_send()
    table_up[3].start()
    for h in range(2):
        hidden_in[h].wait_recv()
        relay[h].start()
    aux_side.wait_recv()
    spread(aux_oth, 1)
    for h in range(2):
        relay[h].wait_recv()
    for i in range(1, 3):
        table_up[i].wait_send()
        table_up[i + 3].start()

    @pl.when(lo == 0)
    def _():
        each_group(lambda start: slope(oth, tab, 1, base_own, s_oth, t_oth, start))
        table_term([(t_own, hid), (t_oth, oth)], GROUP, dwp, BF16)
        for c in by_side + leg_1:
            c.start()
        halve(1, [(s_oth, tab, whole)], False)
        send_other()
        table_term([(t_own, hid), (t_oth, oth)], 0, dwp, BF16)

    @pl.when(lo == 1)
    def _():
        leg_1_odd[0].wait_recv()
        leg_2_odd[0].start()

    for i in range(3, 5):
        table_up[i].wait_send()
        table_up[i + 3].start()

    @pl.when(lo == 1)
    def _():
        leg_1_odd[1].wait_recv()
        leg_2_odd[1].start()

    aux_up.wait_recv()
    base_arr = aux_arr[3:4, 0:1]
    for i in range(4):
        table_up[i].wait_recv()
    slope(hid, arr, 0, base_arr, s_arr, t_arr, 0)

    @pl.when(lo == 0)
    def _():
        begin(0, [(s_own, tab, whole), (s_arr, arr, first)])
        table_term([(t_arr, hid)], 0, grad, F32)

    @pl.when(lo == 1)
    def _():
        slope(oth, arr, 1, base_arr, s_oth, t_oth, 0)
        begin(1, [(s_oth, arr, first)])
        begin(0, [(s_own, tab, whole), (s_arr, arr, first)])
        table_term([(t_arr, hid), (t_oth, oth)], 0, grad, F32)

    @pl.when(lo == 0)
    def _():
        leg_1[0].wait_recv()
        leg_2[0].start()
        for i in range(5, 8):
            table_up[i].wait_send()
        for i in range(3):
            grad_up[i].start()
        leg_1[1].wait_recv()
        leg_2[1].start()

    @pl.when(lo == 1)
    def _():
        spread(aux_arr, 2)
        for i in range(5, 8):
            table_up[i].wait_send()
        for c in hid_up:
            c.start()

    for i in range(4, 8):
        table_up[i].wait_recv()
    slope(hid, arr, 0, base_arr, s_arr, t_arr, GROUP)
    halve(0, [(s_arr, arr, second)], True)
    send_own()

    @pl.when(lo == 1)
    def _():
        slope(oth, arr, 1, base_arr, s_oth, t_oth, GROUP)
        halve(1, [(s_oth, arr, second)], True)
        send_other()
        leg_2_odd[0].wait_recv()
        leg_3_odd[0].start()

    @pl.when(lo == 0)
    def _():
        grad_up[0].wait_send()
        grad_up[3].start()
        table_term([(t_arr, hid)], GROUP, grad, F32)

    @pl.when(lo == 1)
    def _():
        table_term([(t_arr, hid), (t_oth, oth)], GROUP, grad, F32)

    send_rest()

    def finish(cut):
        grad[rows_of(cut)] = grad[rows_of(cut)] + dwr[rows_of(cut)].astype(F32)

    def finish_hidden():
        for h in range(2):
            for late in range(2):
                side_arrival(h, late).wait_recv()
        total = keep[hi] + cc_in[hi].astype(F32) + x_in[0].astype(F32) + x_in[1].astype(F32)
        gh_out[...] = total.astype(BF16)

    @pl.when(lo == 0)
    def _():
        count = len(GRAD_CUTS)
        leg_2[0].wait_recv()
        leg_3[0].start()
        for i in range(count):
            if i + 4 < count:
                grad_up[i + 1].wait_send()
                grad_up[i + 4].start()
            if i == 2:
                leg_2[1].wait_recv()
                leg_3[1].start()
            grad_up[i].wait_recv()
            finish(GRAD_CUTS[i])
        for i in range(2):
            leg_3[i].wait_recv()
            finish(LONG_CUTS[i])
        finish_hidden()
        for j, (h, low, size) in enumerate(SIDE_PARTS):
            by_back_in[j].wait_recv()
            finish((SIDE_CUTS[h][0] + low, size))
        for c in by_side + leg_1 + leg_2 + leg_3 + grad_up[count - 3:]:
            c.wait_send()

    @pl.when(lo == 1)
    def _():
        for c in by_side_in:
            c.wait_recv()
        hid_up[0].wait_send()
        hid_up[1].wait_send()
        by_above[0].start()
        leg_2_odd[1].wait_recv()
        leg_3_odd[1].start()
        hid_up[2].wait_send()
        by_above[1].start()
        for c in hid_up[:3]:
            c.wait_recv()
        hid_relay[0].start()
        for i in range(2):
            leg_3_odd[i].wait_recv()
            hid_relay[2 + i].start()
        hid_up[3].wait_send()
        by_above[2].start()
        by_above[3].start()
        hid_up[3].wait_recv()
        hid_relay[1].start()
        for j in range(2):
            by_above[j].wait_recv()
            by_back[j].start()
        for c in hid_relay:
            c.wait_recv()
        each_group(lambda start: slope(thr, arr, 2, base_arr, None, t_thr, start))
        for j in range(2, 4):
            by_above[j].wait_recv()
            by_back[j].start()
        each_group(lambda start: table_term([(t_thr, thr)], start, grad, F32, more=True))
        finish_hidden()
        for c in leg_1_odd + leg_2_odd + leg_3_odd + hid_relay + by_back + by_above:
            c.wait_send()

    aux_side.wait_send()
    aux_up.wait_send()
    for c in hidden_out + relay:
        c.wait_send()
    for tok in range(2):
        for h in range(2):
            core_copy(tok, h).wait_send()
    for h in range(2):
        cross_arrival(h).wait_send()
        for late in range(2):
            side_arrival(h, late).wait_send()


def per_device(rows_of_ring, hidden, table, targets, group_start, log_norm, loss_grad):
    tokens, width = hidden.shape
    vocab = table.shape[0]
    quarter = tokens // 4
    padded = -(-tokens // 128) * 128
    dma = pltpu.SemaphoreType.DMA
    return pl.pallas_call(
        functools.partial(kernel, rows_of_ring),
        out_shape=(
            pltpu.VMEM((quarter, width), BF16),
            pltpu.VMEM((vocab, width), F32),
        ),
        in_specs=[
            pl.BlockSpec(memory_space=pltpu.VMEM),
            pl.BlockSpec(memory_space=pltpu.SMEM),
            pl.BlockSpec(memory_space=pltpu.VMEM),
            pl.BlockSpec(memory_space=pltpu.VMEM),
            pl.BlockSpec(memory_space=pl.ANY),
            pl.BlockSpec(memory_space=pl.ANY),
        ],
        out_specs=[pl.BlockSpec(memory_space=pltpu.VMEM)] * 2,
        scratch_shapes=[
            *[pltpu.VMEM((tokens, width), BF16)] * 3,
            *[pltpu.VMEM((vocab, width), BF16)] * 2,
            *[pltpu.VMEM((8, padded), F32)] * 3,
            pltpu.VMEM((3, tokens, 128), F32),
            *[pltpu.VMEM((tokens, vocab), BF16)] * 3,
            *[pltpu.VMEM((vocab, tokens), BF16)] * 4,
            *[pltpu.VMEM((vocab, width), BF16)] * 2,
            *[pltpu.VMEM((4, quarter, width), F32)] * 2,
            *[pltpu.VMEM((4, quarter, width), BF16)] * 2,
            pltpu.VMEM((3, quarter, width), BF16),
            pltpu.VMEM((2, quarter, width), BF16),
            pltpu.VMEM((2, quarter, width // 2), BF16),
            *[pltpu.VMEM((LONG_ROWS, width), BF16)] * 2,
            *[pltpu.VMEM((2, SIDE_CUTS[0][1], width), BF16)] * 2,
            dma((2,)), dma((COPIES,)), dma((COPIES,)),
        ],
        compiler_params=pltpu.CompilerParams(
            collective_id=1, has_side_effects=True, vmem_limit_bytes=56 * 2**20
        ),
        cost_estimate=pl.CostEstimate(
            flops=18 * tokens * vocab * width, bytes_accessed=12 * tokens * width, transcendentals=3 * tokens * vocab
        ),
    )(targets, group_start, log_norm, loss_grad, hidden, table)


def solution(mesh):
    placed = (P("blk", None), P(("blk", "vocab"), None), P("blk"), P("blk"), P("blk"), P("blk"))
    return jax.shard_map(
        functools.partial(per_device, mesh.shape["blk"] // 2),
        mesh=mesh,
        in_specs=placed,
        out_specs=(P(("blk", "vocab"), None), P(("blk", "vocab"), None)),
        check_vma=False,
    )
```

```python
import functools

import jax
import jax.numpy as jnp
from jax import lax
from jax.experimental import pallas as pl
from jax.experimental.pallas import tpu as pltpu
from jax.sharding import PartitionSpec as P

MESH = pl.DeviceIdType.MESH
GROUP = 256
WIDE = 768
RING, LEG = 8, 3
TABLE_CUTS = tuple((64 * i, 64) for i in range(8))
GRAD_CUTS = tuple((64 * i, 64) for i in range(5)) + ((320, 48),)
SIDE_CUTS = ((368, 32), (400, 32))
LONG_CUTS = ((432, 48), (480, 32))
SIDE_PARTS = ((0, 0, 32), (1, 0, 32))
LONG_TABLE = (496, 16)
LONG_ROWS = 112
HID_CUTS = ((0, 0, 64), (0, 64, 64), (0, 128, 48), (1, 0, 64))
HID_LONG = ((1, 64, 64), (1, 128, 48))
HID_SHARE = ((0, 0, 176), (1, 0, 64)) + HID_LONG
F32, BF16 = jnp.float32, jnp.bfloat16

AUX, SIDE_HID, SIDE_RELAY, CORE, CROSS, SIDE = 0, 2, 4, 6, 10, 12
TABLE = 16
GRAD = TABLE + len(TABLE_CUTS)
LONG = GRAD + len(GRAD_CUTS)
HID_UP = LONG + 6
HID_RELAY = HID_UP + len(HID_CUTS)
BY_SIDE = HID_RELAY + len(HID_SHARE)
BY_UP = BY_SIDE + 2
BY_BACK = BY_UP + 2
LONG_TAB = BY_BACK + 2
COPIES = LONG_TAB + 3


def kernel(
    rows_of_ring, tgt_ref, first_ref, norm_ref, cot_ref, hid_hbm, tab_hbm, gh_out, grad,
    hid, oth, thr, tab, arr, aux_ref, aux_oth, aux_arr, cols,
    s_own, s_oth, s_arr, t_own, t_oth, t_arr, t_thr,
    dwp, dwr, keep, give, cc_out, cc_in, x_out, x_in, m_in, way_a, way_b, by_in, by_up, lsem, send, recv,
):
    tokens, width = hid.shape
    vocab = tab.shape[0]
    quarter = tokens // 4
    blk, part = lax.axis_index("blk"), lax.axis_index("vocab")
    row, lo = blk // 2, blk % 2
    hi, core = part // 2, part % 2
    plane, height = row // RING, row % RING

    def at(r, low, high, c):
        return (((r + rows_of_ring) % rows_of_ring) * 2 + low, high * 2 + c)

    def along(y, z):
        return y * RING + (z + RING) % RING

    up, down = at(row + 1, lo, hi, core), at(row - 1, lo, hi, core)
    side = [at(row, 1 - lo, h, core) for h in range(2)]
    sibling = at(row, lo, hi, 1 - core)
    turn_to = lax.rem(height + RING + LEG, RING) == RING - 1
    turn_from = lax.rem(height + 2 * LEG, RING) == RING - 1
    leg_to = at(along(plane, height - LEG), lo, hi, core)
    leg_from = at(along(plane, height + LEG), lo, hi, core)
    turn_to = at(along(plane + turn_to.astype(jnp.int32), height - LEG), lo, hi, core)
    turn_from = at(along(plane - turn_from.astype(jnp.int32), height + LEG), lo, hi, core)
    last_to = at(along(plane, height - 1), lo, hi, core)
    last_from = at(along(plane, height + 1), lo, hi, core)

    barrier = pltpu.get_barrier_semaphore()
    partners = (up, down, side[0], side[1], sibling, leg_to, leg_from, turn_to, turn_from, last_to, last_from)
    for device in partners:
        pl.semaphore_signal(barrier, inc=1, device_id=device, device_id_type=MESH)

    load_hid = pltpu.make_async_copy(hid_hbm, hid, lsem.at[0])
    load_tab = pltpu.make_async_copy(tab_hbm, tab, lsem.at[1])
    load_hid.start()
    load_tab.start()

    aux_ref[...] = jnp.zeros_like(aux_ref)
    aux_ref[0:1, :tokens] = tgt_ref[...].astype(F32).reshape(1, tokens)
    aux_ref[1:2, :tokens] = norm_ref[...].reshape(1, tokens)
    aux_ref[2:3, :tokens] = cot_ref[...].reshape(1, tokens)
    aux_ref[3:4, :] = jnp.full((1, aux_ref.shape[1]), first_ref[0].astype(F32), F32)

    pl.semaphore_wait(barrier, len(partners))

    def quarter_of(h, c):
        return pl.ds(pl.multiple_of((h * 2 + c) * quarter, 16), quarter)

    def rows_of(cut):
        return pl.ds(cut[0], cut[1])

    def copy(src, dst, number, device, number_there=None):
        there = number if number_there is None else number_there
        return pltpu.make_async_remote_copy(
            src_ref=src, dst_ref=dst, send_sem=send.at[number], recv_sem=recv.at[there],
            device_id=device, device_id_type=MESH,
        )

    table_up = [copy(tab_hbm.at[rows_of(c)], arr.at[rows_of(c)], TABLE + i, up) for i, c in enumerate(TABLE_CUTS)]
    grad_up = [copy(dwp.at[rows_of(c)], dwr.at[rows_of(c)], GRAD + i, up) for i, c in enumerate(GRAD_CUTS)]

    def piece_of(cut):
        return pl.ds(pl.multiple_of((cut[0] * 2 + core) * quarter + cut[1], 16), cut[2])

    def legs(sources, targets, sizes):
        first, second, third, place = [], [], [], 0
        for i, (source, target, size) in enumerate(zip(sources, targets, sizes)):
            stop = pl.ds(place, size)
            first.append(copy(source, way_a.at[stop], LONG + i, leg_to))
            second.append(copy(way_a.at[stop], way_b.at[stop], LONG + 2 + i, turn_to))
            third.append(copy(way_b.at[stop], target, LONG + 4 + i, last_to))
            place += size
        return first, second, third

    leg_1, leg_2, leg_3 = legs(
        [dwp.at[rows_of(c)] for c in LONG_CUTS], [dwr.at[rows_of(c)] for c in LONG_CUTS], [c[1] for c in LONG_CUTS]
    )
    leg_1_odd, leg_2_odd, leg_3_odd = legs(
        [hid_hbm.at[piece_of(h)] for h in HID_LONG], [thr.at[piece_of(h)] for h in HID_LONG], [h[2] for h in HID_LONG]
    )

    last = TABLE_CUTS[-1][0]
    rest = pl.ds(last, LONG_TABLE[0] - last)
    table_last = copy(tab_hbm.at[rest], arr.at[rest], TABLE + len(TABLE_CUTS) - 1, up)
    spare = pl.ds(LONG_ROWS - LONG_TABLE[1], LONG_TABLE[1])
    table_1 = copy(tab_hbm.at[rows_of(LONG_TABLE)], way_a.at[spare], LONG_TAB, leg_to)
    table_2 = copy(way_a.at[spare], way_b.at[spare], LONG_TAB + 1, turn_to)
    table_3 = copy(way_b.at[spare], arr.at[rows_of(LONG_TABLE)], LONG_TAB + 2, last_to)

    hid_up = [copy(hid_hbm.at[piece_of(h)], thr.at[piece_of(h)], HID_UP + i, up) for i, h in enumerate(HID_CUTS)]
    hid_relay = [copy(thr.at[piece_of(h)], thr.at[piece_of(h)], HID_RELAY + i, sibling) for i, h in enumerate(HID_SHARE)]

    by_side = [copy(dwp.at[rows_of(c)], by_in.at[hi], BY_SIDE + g, side[g], BY_SIDE + hi) for g, c in enumerate(SIDE_CUTS)]
    by_side_in = [copy(by_in.at[h], by_in.at[h], BY_SIDE + h, side[h]) for h in range(2)]
    by_above, by_back, by_back_in = [], [], []
    for j, (h, low, size) in enumerate(SIDE_PARTS):
        there = SIDE_CUTS[0][0] + low
        rows = pl.ds(low, size)
        back = pl.ds(pl.multiple_of(there + hi * SIDE_CUTS[0][1], 16), size)
        by_above.append(copy(by_in.at[h, rows], by_up.at[h, rows], BY_UP + j, up))
        by_back.append(copy(by_up.at[h, rows], dwr.at[back], BY_BACK + j, side[h], BY_BACK + 2 * (j // 2) + hi))
        landed = pl.ds(there + h * SIDE_CUTS[0][1], size)
        by_back_in.append(copy(by_up.at[h, rows], dwr.at[landed], BY_BACK + j, side[h]))

    mine = quarter_of(hi, core)
    hidden_out = [copy(hid_hbm.at[mine], oth.at[mine], SIDE_HID + h, side[h], SIDE_HID + hi) for h in range(2)]
    hidden_in = [copy(oth.at[quarter_of(h, core)], oth.at[quarter_of(h, core)], SIDE_HID + h, side[h]) for h in range(2)]
    relay = [copy(oth.at[quarter_of(h, core)], oth.at[quarter_of(h, core)], SIDE_RELAY + h, sibling) for h in range(2)]
    aux_side = copy(aux_ref, aux_oth, AUX, at(row, 1 - lo, hi, core))
    aux_up = copy(aux_ref, aux_arr, AUX + 1, up)

    aux_side.start()
    for c in hidden_out:
        c.start()
    aux_up.start()
    for i in range(3):
        table_up[i].start()

    @pl.when(lo == 0)
    def _():
        table_1.start()

    @pl.when(lo == 1)
    def _():
        for c in leg_1_odd:
            c.start()

    def spread(ref, slot):
        for i in range(ref.shape[1] // 128):
            block = ref[:, i * 128:(i + 1) * 128]
            square = jnp.concatenate([block] * 16, axis=0)
            rest = min(128, tokens - i * 128)
            cols[slot, i * 128:i * 128 + rest, :] = square.T[:rest]

    def slope_of(hid_rows, tab_rows, slot, rows, base, start):
        logits = lax.dot_general(
            hid_rows, tab_rows, (((1,), (1,)), ((), ())), preferred_element_type=F32
        )
        ids = (lax.broadcasted_iota(jnp.int32, (1, GROUP), 1) + (part * vocab + start)).astype(F32)
        hit = (cols[slot, rows, 0:1] == base + ids).astype(F32)
        return cols[slot, rows, 2:3] * (jnp.exp(logits - cols[slot, rows, 1:2]) - hit)

    def slope(hid_ref, tab_ref, slot, base, out, out_t, start):
        group = pl.ds(start, GROUP)
        value = slope_of(hid_ref[...], tab_ref[group, :], slot, pl.ds(0, tokens), base, start)
        out[:, group] = value.astype(BF16)
        out_t[group, :] = value.T.astype(BF16)

    def each_group(body):
        def step(i, carry):
            body(pl.multiple_of(i * GROUP, GROUP))
            return carry
        lax.fori_loop(0, vocab // GROUP, step, 0)

    def each_wide(body):
        def step(i, carry):
            body(pl.ds(pl.multiple_of(i * WIDE, WIDE), WIDE))
            return carry
        lax.fori_loop(0, width // WIDE, step, 0)

    def table_term(terms, start, out, dtype):
        group = pl.ds(start, GROUP)

        def body(wide):
            total = None
            for st, h in terms:
                term = jnp.dot(st[group, :], h[:, wide], preferred_element_type=F32)
                total = term if total is None else total + term
            out[group, wide] = total.astype(dtype)
        each_wide(body)

    def hidden_term(terms, rows, store):
        def body(wide):
            total = None
            for s, t, span in terms:
                term = jnp.dot(s[rows, span], t[span, wide], preferred_element_type=F32)
                total = term if total is None else total + term
            store(wide, total)
        each_wide(body)

    def core_copy(tok, h):
        slot = tok * 2 + h
        return copy(cc_out.at[slot], cc_in.at[slot], CORE + slot, sibling)

    def begin(tok, terms):
        for h in range(2):
            for c, place in ((1 - core, give), (core, keep)):
                def put(wide, value, place=place, slot=tok * 2 + h):
                    place[slot, :, wide] = value
                hidden_term(terms, quarter_of(h, c), put)

    def halve(tok, terms, begun):
        for h in range(2):
            def put(wide, value, slot=tok * 2 + h):
                if begun:
                    value = value + give[slot, :, wide]
                cc_out[slot, :, wide] = value.astype(BF16)
            hidden_term(terms, quarter_of(h, 1 - core), put)
            core_copy(tok, h).start()
        for h in range(2):
            def put(wide, value, slot=tok * 2 + h):
                if begun:
                    value = value + keep[slot, :, wide]
                keep[slot, :, wide] = value
            hidden_term(terms, quarter_of(h, core), put)

    half = width // 2

    def columns(g):
        return pl.ds(pl.multiple_of(g * half, 128), half)

    def cross_copy(g):
        return copy(x_out.at[0, :, columns(g)], m_in.at[hi], CROSS + g, side[g], CROSS + hi)

    def cross_arrival(g):
        return copy(x_out.at[0, :, columns(g)], m_in.at[g], CROSS + g, side[g])

    def side_copy(h, late):
        span = columns(hi if late else 1 - hi)
        return copy(
            x_out.at[1 + h, :, span], x_in.at[hi, :, span], SIDE + 2 * h + late, side[h], SIDE + 2 * hi + late
        )

    def side_arrival(h, late):
        span = columns(h if late else 1 - h)
        return copy(x_out.at[1 + h, :, span], x_in.at[h, :, span], SIDE + 2 * h + late, side[h])

    def send_own():
        for h in range(2):
            core_copy(0, h).wait_recv()
        x_out[0] = (keep[1 - hi] + cc_in[1 - hi].astype(F32)).astype(BF16)
        for g in range(2):
            cross_copy(g).start()

    def send_other():
        for h in range(2):
            core_copy(1, h).wait_recv()
            span = columns(1 - hi)
            x_out[1 + h, :, span] = (keep[2 + h, :, span] + cc_in[2 + h, :, span].astype(F32)).astype(BF16)
            side_copy(h, 0).start()

    def send_rest():
        for h in range(2):
            cross_arrival(1 - h).wait_recv()
            span = columns(hi)
            value = keep[2 + h, :, span] + cc_in[2 + h, :, span].astype(F32) + m_in[1 - h].astype(F32)
            x_out[1 + h, :, span] = value.astype(BF16)
            side_copy(h, 1).start()

    whole, first, second = pl.ds(0, vocab), pl.ds(0, GROUP), pl.ds(GROUP, GROUP)

    spread(aux_ref, 0)
    load_hid.wait()
    load_tab.wait()
    base_own = aux_ref[3:4, 0:1]
    each_group(lambda start: slope(hid, tab, 0, base_own, s_own, t_own, start))

    table_up[0].wait_send()
    table_up[3].start()
    for h in range(2):
        hidden_in[h].wait_recv()
        relay[h].start()
    aux_side.wait_recv()
    spread(aux_oth, 1)
    for h in range(2):
        relay[h].wait_recv()
    for i in range(1, 3):
        table_up[i].wait_send()
        table_up[i + 3].start()

    @pl.when(lo == 0)
    def _():
        table_1.wait_recv()
        table_2.start()
        each_group(lambda start: slope(oth, tab, 1, base_own, s_oth, t_oth, start))
        table_term([(t_own, hid), (t_oth, oth)], GROUP, dwp, BF16)
        for c in by_side + leg_1:
            c.start()
        halve(1, [(s_oth, tab, whole)], False)
        send_other()
        table_term([(t_own, hid), (t_oth, oth)], 0, dwp, BF16)
        table_2.wait_recv()
        table_3.start()

    @pl.when(lo == 1)
    def _():
        leg_1_odd[0].wait_recv()
        leg_2_odd[0].start()

    table_up[3].wait_send()
    table_up[6].start()
    table_up[4].wait_send()

    @pl.when(lo == 0)
    def _():
        table_last.start()

    @pl.when(lo == 1)
    def _():
        table_up[7].start()


    @pl.when(lo == 1)
    def _():
        leg_1_odd[1].wait_recv()
        leg_2_odd[1].start()

    aux_up.wait_recv()
    base_arr = aux_arr[3:4, 0:1]
    for i in range(4):
        table_up[i].wait_recv()
    slope(hid, arr, 0, base_arr, s_arr, t_arr, 0)

    @pl.when(lo == 0)
    def _():
        begin(0, [(s_own, tab, whole), (s_arr, arr, first)])
        table_term([(t_arr, hid)], 0, grad, F32)

    @pl.when(lo == 1)
    def _():
        slope(oth, arr, 1, base_arr, s_oth, t_oth, 0)
        begin(1, [(s_oth, arr, first)])
        begin(0, [(s_own, tab, whole), (s_arr, arr, first)])
        table_term([(t_arr, hid), (t_oth, oth)], 0, grad, F32)

    @pl.when(lo == 0)
    def _():
        leg_1[0].wait_recv()
        leg_2[0].start()
        for i in range(5, 7):
            table_up[i].wait_send()
        table_last.wait_send()
        for i in range(3):
            grad_up[i].start()
        leg_1[1].wait_recv()
        leg_2[1].start()

    @pl.when(lo == 1)
    def _():
        spread(aux_arr, 2)
        for i in range(5, 8):
            table_up[i].wait_send()
        for c in by_side_in:
            c.wait_recv()
        for c in (hid_up[0], hid_up[1], by_above[0], by_above[1]):
            c.start()

    for i in range(4, 7):
        table_up[i].wait_recv()

    @pl.when(lo == 0)
    def _():
        table_last.wait_recv()
        table_3.wait_recv()

    @pl.when(lo == 1)
    def _():
        table_up[7].wait_recv()

    slope(hid, arr, 0, base_arr, s_arr, t_arr, GROUP)
    halve(0, [(s_arr, arr, second)], True)
    send_own()

    @pl.when(lo == 1)
    def _():
        slope(oth, arr, 1, base_arr, s_oth, t_oth, GROUP)
        halve(1, [(s_oth, arr, second)], True)
        send_other()
        hid_up[2].start()
        leg_2_odd[0].wait_recv()
        leg_3_odd[0].start()

    @pl.when(lo == 0)
    def _():
        grad_up[0].wait_send()
        grad_up[3].start()
        table_term([(t_arr, hid)], GROUP, grad, F32)

    @pl.when(lo == 1)
    def _():
        table_term([(t_arr, hid), (t_oth, oth)], GROUP, grad, F32)

    send_rest()

    def finish(cut):
        grad[rows_of(cut)] = grad[rows_of(cut)] + dwr[rows_of(cut)].astype(F32)

    def finish_hidden():
        for h in range(2):
            for late in range(2):
                side_arrival(h, late).wait_recv()
        total = keep[hi] + cc_in[hi].astype(F32) + x_in[0].astype(F32) + x_in[1].astype(F32)
        gh_out[...] = total.astype(BF16)

    @pl.when(lo == 0)
    def _():
        count = len(GRAD_CUTS)
        leg_2[0].wait_recv()
        leg_3[0].start()
        for i in range(count):
            if i + 4 < count:
                grad_up[i + 1].wait_send()
                grad_up[i + 4].start()
            if i == 2:
                leg_2[1].wait_recv()
                leg_3[1].start()
            grad_up[i].wait_recv()
            finish(GRAD_CUTS[i])
        for i in range(2):
            leg_3[i].wait_recv()
            finish(LONG_CUTS[i])
        finish_hidden()
        for j, (h, low, size) in enumerate(SIDE_PARTS):
            by_back_in[j].wait_recv()
            finish((SIDE_CUTS[h][0] + low, size))
        for c in [table_1, table_2, table_3] + by_side + leg_1 + leg_2 + leg_3 + grad_up[count - 3:]:
            c.wait_send()

    def half_term(n):
        rows = pl.ds(n * 2 * quarter, 2 * quarter)

        def step(start):
            group = pl.ds(start, GROUP)
            value = slope_of(thr[rows, :], arr[group, :], 2, rows, base_arr, start)
            t_thr[n, group, :] = value.T.astype(BF16)

            def body(wide):
                grad[group, wide] += jnp.dot(t_thr[n, group, :], thr[rows, wide], preferred_element_type=F32)
            each_wide(body)
        each_group(step)

    @pl.when(lo == 1)
    def _():
        hid_up[3].start()
        leg_2_odd[1].wait_recv()
        leg_3_odd[1].start()
        for j in range(2):
            by_above[j].wait_recv()
            by_back[j].start()
        for c in hid_up[:3]:
            c.wait_recv()
        hid_relay[0].start()
        hid_relay[0].wait_recv()
        half_term(0)
        for i in range(2):
            leg_3_odd[i].wait_recv()
            hid_relay[2 + i].start()
        finish_hidden()
        hid_up[3].wait_recv()
        hid_relay[1].start()
        for c in hid_relay[1:]:
            c.wait_recv()
        half_term(1)
        for c in hid_up:
            c.wait_send()
        for c in leg_1_odd + leg_2_odd + leg_3_odd + hid_relay + by_back + by_above:
            c.wait_send()

    aux_side.wait_send()
    aux_up.wait_send()
    for c in hidden_out + relay:
        c.wait_send()
    for tok in range(2):
        for h in range(2):
            core_copy(tok, h).wait_send()
    for h in range(2):
        cross_arrival(h).wait_send()
        for late in range(2):
            side_arrival(h, late).wait_send()


def per_device(rows_of_ring, hidden, table, targets, group_start, log_norm, loss_grad):
    tokens, width = hidden.shape
    vocab = table.shape[0]
    quarter = tokens // 4
    padded = -(-tokens // 128) * 128
    dma = pltpu.SemaphoreType.DMA
    return pl.pallas_call(
        functools.partial(kernel, rows_of_ring),
        out_shape=(
            pltpu.VMEM((quarter, width), BF16),
            pltpu.VMEM((vocab, width), F32),
        ),
        in_specs=[
            pl.BlockSpec(memory_space=pltpu.VMEM),
            pl.BlockSpec(memory_space=pltpu.SMEM),
            pl.BlockSpec(memory_space=pltpu.VMEM),
            pl.BlockSpec(memory_space=pltpu.VMEM),
            pl.BlockSpec(memory_space=pl.ANY),
            pl.BlockSpec(memory_space=pl.ANY),
        ],
        out_specs=[pl.BlockSpec(memory_space=pltpu.VMEM)] * 2,
        scratch_shapes=[
            *[pltpu.VMEM((tokens, width), BF16)] * 3,
            *[pltpu.VMEM((vocab, width), BF16)] * 2,
            *[pltpu.VMEM((8, padded), F32)] * 3,
            pltpu.VMEM((3, tokens, 128), F32),
            *[pltpu.VMEM((tokens, vocab), BF16)] * 3,
            *[pltpu.VMEM((vocab, tokens), BF16)] * 3,
            pltpu.VMEM((2, vocab, tokens // 2), BF16),
            *[pltpu.VMEM((vocab, width), BF16)] * 2,
            *[pltpu.VMEM((4, quarter, width), F32)] * 2,
            *[pltpu.VMEM((4, quarter, width), BF16)] * 2,
            pltpu.VMEM((3, quarter, width), BF16),
            pltpu.VMEM((2, quarter, width), BF16),
            pltpu.VMEM((2, quarter, width // 2), BF16),
            *[pltpu.VMEM((LONG_ROWS, width), BF16)] * 2,
            *[pltpu.VMEM((2, SIDE_CUTS[0][1], width), BF16)] * 2,
            dma((2,)), dma((COPIES,)), dma((COPIES,)),
        ],
        compiler_params=pltpu.CompilerParams(
            collective_id=1, has_side_effects=True, vmem_limit_bytes=56 * 2**20
        ),
        cost_estimate=pl.CostEstimate(
            flops=18 * tokens * vocab * width, bytes_accessed=12 * tokens * width, transcendentals=3 * tokens * vocab
        ),
    )(targets, group_start, log_norm, loss_grad, hidden, table)


def solution(mesh):
    placed = (P("blk", None), P(("blk", "vocab"), None), P("blk"), P("blk"), P("blk"), P("blk"))
    return jax.shard_map(
        functools.partial(per_device, mesh.shape["blk"] // 2),
        mesh=mesh,
        in_specs=placed,
        out_specs=(P(("blk", "vocab"), None), P(("blk", "vocab"), None)),
        check_vma=False,
    )
```

```python
import functools

import jax
import jax.numpy as jnp
from jax import lax
from jax.experimental import pallas as pl
from jax.experimental.pallas import tpu as pltpu
from jax.sharding import PartitionSpec as P

MESH = pl.DeviceIdType.MESH
GROUP = 256
WIDE = 768
RING, LEG = 8, 3
TABLE_CUTS = tuple((64 * i, 64) for i in range(8))
GRAD_CUTS = tuple((64 * i, 64) for i in range(5)) + ((320, 48),)
SIDE_CUTS = ((368, 32), (400, 32))
LONG_CUTS = ((432, 48), (480, 32))
SIDE_PARTS = ((0, 0, 32), (1, 0, 32))
LONG_TABLE = (496, 16)
LONG_ROWS = 112
HID_CUTS = ((0, 0, 64), (0, 64, 64), (0, 128, 48), (1, 0, 64))
HID_LONG = ((1, 64, 64), (1, 128, 48))
HID_SHARE = ((0, 0, 176), (1, 0, 64)) + HID_LONG
F32, BF16 = jnp.float32, jnp.bfloat16

AUX, SIDE_HID, SIDE_RELAY, CORE, CROSS, SIDE = 0, 2, 4, 6, 10, 12
TABLE = 16
GRAD = TABLE + len(TABLE_CUTS)
LONG = GRAD + len(GRAD_CUTS)
HID_UP = LONG + 6
HID_RELAY = HID_UP + len(HID_CUTS)
BY_SIDE = HID_RELAY + len(HID_SHARE)
BY_UP = BY_SIDE + 2
BY_BACK = BY_UP + 2
LONG_TAB = BY_BACK + 2
COPIES = LONG_TAB + 3


def kernel(
    rows_of_ring, tgt_ref, first_ref, norm_ref, cot_ref, hid_hbm, tab_hbm, gh_out, grad,
    hid, oth, thr, tab, arr, aux_ref, aux_oth, aux_arr, cols,
    s_own, s_oth, s_arr, t_own, t_oth, t_arr, t_thr,
    dwp, dwr, keep, give, cc_out, cc_in, x_out, x_in, m_in, way_a, way_b, by_in, by_up, lsem, send, recv,
):
    tokens, width = hid.shape
    vocab = tab.shape[0]
    quarter = tokens // 4
    blk, part = lax.axis_index("blk"), lax.axis_index("vocab")
    row, lo = blk // 2, blk % 2
    hi, core = part // 2, part % 2
    plane, height = row // RING, row % RING

    def at(r, low, high, c):
        return (((r + rows_of_ring) % rows_of_ring) * 2 + low, high * 2 + c)

    def along(y, z):
        return y * RING + (z + RING) % RING

    up, down = at(row + 1, lo, hi, core), at(row - 1, lo, hi, core)
    side = [at(row, 1 - lo, h, core) for h in range(2)]
    sibling = at(row, lo, hi, 1 - core)
    turn_to = lax.rem(height + RING + LEG, RING) == RING - 1
    turn_from = lax.rem(height + 2 * LEG, RING) == RING - 1
    leg_to = at(along(plane, height - LEG), lo, hi, core)
    leg_from = at(along(plane, height + LEG), lo, hi, core)
    turn_to = at(along(plane + turn_to.astype(jnp.int32), height - LEG), lo, hi, core)
    turn_from = at(along(plane - turn_from.astype(jnp.int32), height + LEG), lo, hi, core)
    last_to = at(along(plane, height - 1), lo, hi, core)
    last_from = at(along(plane, height + 1), lo, hi, core)

    barrier = pltpu.get_barrier_semaphore()
    partners = (up, down, side[0], side[1], sibling, leg_to, leg_from, turn_to, turn_from, last_to, last_from)
    for device in partners:
        pl.semaphore_signal(barrier, inc=1, device_id=device, device_id_type=MESH)

    load_hid = pltpu.make_async_copy(hid_hbm, hid, lsem.at[0])
    load_tab = pltpu.make_async_copy(tab_hbm, tab, lsem.at[1])
    load_hid.start()
    load_tab.start()

    aux_ref[...] = jnp.zeros_like(aux_ref)
    aux_ref[0:1, :tokens] = tgt_ref[...].astype(F32).reshape(1, tokens)
    aux_ref[1:2, :tokens] = norm_ref[...].reshape(1, tokens)
    aux_ref[2:3, :tokens] = cot_ref[...].reshape(1, tokens)
    aux_ref[3:4, :] = jnp.full((1, aux_ref.shape[1]), first_ref[0].astype(F32), F32)

    pl.semaphore_wait(barrier, len(partners))

    def quarter_of(h, c):
        return pl.ds(pl.multiple_of((h * 2 + c) * quarter, 16), quarter)

    def rows_of(cut):
        return pl.ds(cut[0], cut[1])

    def copy(src, dst, number, device, number_there=None):
        there = number if number_there is None else number_there
        return pltpu.make_async_remote_copy(
            src_ref=src, dst_ref=dst, send_sem=send.at[number], recv_sem=recv.at[there],
            device_id=device, device_id_type=MESH,
        )

    table_up = [copy(tab_hbm.at[rows_of(c)], arr.at[rows_of(c)], TABLE + i, up) for i, c in enumerate(TABLE_CUTS)]
    grad_up = [copy(dwp.at[rows_of(c)], dwr.at[rows_of(c)], GRAD + i, up) for i, c in enumerate(GRAD_CUTS)]

    def piece_of(cut):
        return pl.ds(pl.multiple_of((cut[0] * 2 + core) * quarter + cut[1], 16), cut[2])

    def legs(sources, targets, sizes):
        first, second, third, place = [], [], [], 0
        for i, (source, target, size) in enumerate(zip(sources, targets, sizes)):
            stop = pl.ds(place, size)
            first.append(copy(source, way_a.at[stop], LONG + i, leg_to))
            second.append(copy(way_a.at[stop], way_b.at[stop], LONG + 2 + i, turn_to))
            third.append(copy(way_b.at[stop], target, LONG + 4 + i, last_to))
            place += size
        return first, second, third

    leg_1, leg_2, leg_3 = legs(
        [dwp.at[rows_of(c)] for c in LONG_CUTS], [dwr.at[rows_of(c)] for c in LONG_CUTS], [c[1] for c in LONG_CUTS]
    )
    leg_1_odd, leg_2_odd, leg_3_odd = legs(
        [hid_hbm.at[piece_of(h)] for h in HID_LONG], [thr.at[piece_of(h)] for h in HID_LONG], [h[2] for h in HID_LONG]
    )

    last = TABLE_CUTS[-1][0]
    rest = pl.ds(last, LONG_TABLE[0] - last)
    table_last = copy(tab_hbm.at[rest], arr.at[rest], TABLE + len(TABLE_CUTS) - 1, up)
    spare = pl.ds(LONG_ROWS - LONG_TABLE[1], LONG_TABLE[1])
    table_1 = copy(tab_hbm.at[rows_of(LONG_TABLE)], way_a.at[spare], LONG_TAB, leg_to)
    table_2 = copy(way_a.at[spare], way_b.at[spare], LONG_TAB + 1, turn_to)
    table_3 = copy(way_b.at[spare], arr.at[rows_of(LONG_TABLE)], LONG_TAB + 2, last_to)

    hid_up = [copy(hid_hbm.at[piece_of(h)], thr.at[piece_of(h)], HID_UP + i, up) for i, h in enumerate(HID_CUTS)]
    hid_relay = [copy(thr.at[piece_of(h)], thr.at[piece_of(h)], HID_RELAY + i, sibling) for i, h in enumerate(HID_SHARE)]

    by_side = [copy(dwp.at[rows_of(c)], by_in.at[hi], BY_SIDE + g, side[g], BY_SIDE + hi) for g, c in enumerate(SIDE_CUTS)]
    by_side_in = [copy(by_in.at[h], by_in.at[h], BY_SIDE + h, side[h]) for h in range(2)]
    by_above, by_back, by_back_in = [], [], []
    for j, (h, low, size) in enumerate(SIDE_PARTS):
        there = SIDE_CUTS[0][0] + low
        rows = pl.ds(low, size)
        back = pl.ds(pl.multiple_of(there + hi * SIDE_CUTS[0][1], 16), size)
        by_above.append(copy(by_in.at[h, rows], by_up.at[h, rows], BY_UP + j, up))
        by_back.append(copy(by_up.at[h, rows], dwr.at[back], BY_BACK + j, side[h], BY_BACK + 2 * (j // 2) + hi))
        landed = pl.ds(there + h * SIDE_CUTS[0][1], size)
        by_back_in.append(copy(by_up.at[h, rows], dwr.at[landed], BY_BACK + j, side[h]))

    mine = quarter_of(hi, core)
    hidden_out = [copy(hid_hbm.at[mine], oth.at[mine], SIDE_HID + h, side[h], SIDE_HID + hi) for h in range(2)]
    hidden_in = [copy(oth.at[quarter_of(h, core)], oth.at[quarter_of(h, core)], SIDE_HID + h, side[h]) for h in range(2)]
    relay = [copy(oth.at[quarter_of(h, core)], oth.at[quarter_of(h, core)], SIDE_RELAY + h, sibling) for h in range(2)]
    aux_side = copy(aux_ref, aux_oth, AUX, at(row, 1 - lo, hi, core))
    aux_up = copy(aux_ref, aux_arr, AUX + 1, up)

    aux_side.start()
    for c in hidden_out:
        c.start()
    aux_up.start()
    for i in range(3):
        table_up[i].start()

    @pl.when(lo == 0)
    def _():
        table_1.start()

    @pl.when(lo == 1)
    def _():
        for c in leg_1_odd:
            c.start()

    def spread(ref, slot):
        for i in range(ref.shape[1] // 128):
            block = ref[:, i * 128:(i + 1) * 128]
            square = jnp.concatenate([block] * 16, axis=0)
            rest = min(128, tokens - i * 128)
            cols[slot, i * 128:i * 128 + rest, :] = square.T[:rest]

    def slope_of(hid_rows, tab_rows, slot, rows, base, start):
        logits = lax.dot_general(
            hid_rows, tab_rows, (((1,), (1,)), ((), ())), preferred_element_type=F32
        )
        ids = (lax.broadcasted_iota(jnp.int32, (1, GROUP), 1) + (part * vocab + start)).astype(F32)
        hit = (cols[slot, rows, 0:1] == base + ids).astype(F32)
        return cols[slot, rows, 2:3] * (jnp.exp(logits - cols[slot, rows, 1:2]) - hit)

    def slope(hid_ref, tab_ref, slot, base, out, out_t, start):
        group = pl.ds(start, GROUP)
        value = slope_of(hid_ref[...], tab_ref[group, :], slot, pl.ds(0, tokens), base, start)
        out[:, group] = value.astype(BF16)
        out_t[group, :] = value.T.astype(BF16)

    def each_group(body):
        def step(i, carry):
            body(pl.multiple_of(i * GROUP, GROUP))
            return carry
        lax.fori_loop(0, vocab // GROUP, step, 0)

    def each_wide(body):
        def step(i, carry):
            body(pl.ds(pl.multiple_of(i * WIDE, WIDE), WIDE))
            return carry
        lax.fori_loop(0, width // WIDE, step, 0)

    def table_term(terms, start, out, dtype):
        group = pl.ds(start, GROUP)

        def body(wide):
            total = None
            for st, h in terms:
                term = jnp.dot(st[group, :], h[:, wide], preferred_element_type=F32)
                total = term if total is None else total + term
            out[group, wide] = total.astype(dtype)
        each_wide(body)

    def hidden_term(terms, rows, store):
        def body(wide):
            total = None
            for s, t, span in terms:
                term = jnp.dot(s[rows, span], t[span, wide], preferred_element_type=F32)
                total = term if total is None else total + term
            store(wide, total)
        each_wide(body)

    def core_copy(tok, h):
        slot = tok * 2 + h
        return copy(cc_out.at[slot], cc_in.at[slot], CORE + slot, sibling)

    def begin(tok, terms):
        for h in range(2):
            for c, place in ((1 - core, give), (core, keep)):
                def put(wide, value, place=place, slot=tok * 2 + h):
                    place[slot, :, wide] = value
                hidden_term(terms, quarter_of(h, c), put)

    def halve(tok, terms, begun):
        for h in range(2):
            def put(wide, value, slot=tok * 2 + h):
                if begun:
                    value = value + give[slot, :, wide]
                cc_out[slot, :, wide] = value.astype(BF16)
            hidden_term(terms, quarter_of(h, 1 - core), put)
            core_copy(tok, h).start()
        for h in range(2):
            def put(wide, value, slot=tok * 2 + h):
                if begun:
                    value = value + keep[slot, :, wide]
                keep[slot, :, wide] = value
            hidden_term(terms, quarter_of(h, core), put)

    half = width // 2

    def columns(g):
        return pl.ds(pl.multiple_of(g * half, 128), half)

    def cross_copy(g):
        return copy(x_out.at[0, :, columns(g)], m_in.at[hi], CROSS + g, side[g], CROSS + hi)

    def cross_arrival(g):
        return copy(x_out.at[0, :, columns(g)], m_in.at[g], CROSS + g, side[g])

    def side_copy(h, late):
        span = columns(hi if late else 1 - hi)
        return copy(
            x_out.at[1 + h, :, span], x_in.at[hi, :, span], SIDE + 2 * h + late, side[h], SIDE + 2 * hi + late
        )

    def side_arrival(h, late):
        span = columns(h if late else 1 - h)
        return copy(x_out.at[1 + h, :, span], x_in.at[h, :, span], SIDE + 2 * h + late, side[h])

    def halve_own(terms):
        def share(h):
            def put(wide, value):
                cc_out[h, :, wide] = (value + give[h, :, wide]).astype(BF16)
            hidden_term(terms, quarter_of(h, 1 - core), put)
            core_copy(0, h).start()

        def hold(h):
            def put(wide, value):
                keep[h, :, wide] = value + keep[h, :, wide]
            hidden_term(terms, quarter_of(h, core), put)

        share(1 - hi)
        hold(1 - hi)
        share(hi)
        core_copy(0, 1 - hi).wait_recv()
        x_out[0] = (keep[1 - hi] + cc_in[1 - hi].astype(F32)).astype(BF16)
        for g in range(2):
            cross_copy(g).start()
        hold(hi)

    def send_other():
        for h in range(2):
            core_copy(1, h).wait_recv()
            span = columns(1 - hi)
            x_out[1 + h, :, span] = (keep[2 + h, :, span] + cc_in[2 + h, :, span].astype(F32)).astype(BF16)
            side_copy(h, 0).start()

    def send_rest():
        for h in range(2):
            cross_arrival(1 - h).wait_recv()
            span = columns(hi)
            value = keep[2 + h, :, span] + cc_in[2 + h, :, span].astype(F32) + m_in[1 - h].astype(F32)
            x_out[1 + h, :, span] = value.astype(BF16)
            side_copy(h, 1).start()

    whole, first, second = pl.ds(0, vocab), pl.ds(0, GROUP), pl.ds(GROUP, GROUP)

    spread(aux_ref, 0)
    load_hid.wait()
    load_tab.wait()
    base_own = aux_ref[3:4, 0:1]
    each_group(lambda start: slope(hid, tab, 0, base_own, s_own, t_own, start))

    table_up[0].wait_send()
    table_up[3].start()
    for h in range(2):
        hidden_in[h].wait_recv()
        relay[h].start()
    aux_side.wait_recv()
    spread(aux_oth, 1)
    for h in range(2):
        relay[h].wait_recv()
    for i in range(1, 3):
        table_up[i].wait_send()
        table_up[i + 3].start()

    @pl.when(lo == 0)
    def _():
        table_1.wait_recv()
        table_2.start()
        each_group(lambda start: slope(oth, tab, 1, base_own, s_oth, t_oth, start))
        table_term([(t_own, hid), (t_oth, oth)], GROUP, dwp, BF16)
        table_2.wait_recv()
        table_3.start()
        for c in by_side + leg_1:
            c.start()
        halve(1, [(s_oth, tab, whole)], False)
        send_other()
        table_term([(t_own, hid), (t_oth, oth)], 0, dwp, BF16)

    @pl.when(lo == 1)
    def _():
        leg_1_odd[0].wait_recv()
        leg_2_odd[0].start()

    table_up[3].wait_send()
    table_up[6].start()
    table_up[4].wait_send()

    @pl.when(lo == 0)
    def _():
        table_last.start()

    @pl.when(lo == 1)
    def _():
        table_up[7].start()


    @pl.when(lo == 1)
    def _():
        leg_1_odd[1].wait_recv()
        leg_2_odd[1].start()

    aux_up.wait_recv()
    base_arr = aux_arr[3:4, 0:1]
    for i in range(4):
        table_up[i].wait_recv()
    slope(hid, arr, 0, base_arr, s_arr, t_arr, 0)

    @pl.when(lo == 0)
    def _():
        begin(0, [(s_own, tab, whole), (s_arr, arr, first)])
        table_term([(t_arr, hid)], 0, grad, F32)

    @pl.when(lo == 1)
    def _():
        slope(oth, arr, 1, base_arr, s_oth, t_oth, 0)
        begin(1, [(s_oth, arr, first)])
        begin(0, [(s_own, tab, whole), (s_arr, arr, first)])
        table_term([(t_arr, hid), (t_oth, oth)], 0, grad, F32)

    @pl.when(lo == 0)
    def _():
        leg_1[0].wait_recv()
        leg_2[0].start()
        for i in range(5, 7):
            table_up[i].wait_send()
        table_last.wait_send()
        for i in range(3):
            grad_up[i].start()

    @pl.when(lo == 1)
    def _():
        spread(aux_arr, 2)
        for i in range(5, 8):
            table_up[i].wait_send()
        for c in by_side_in:
            c.wait_recv()
        for c in (hid_up[0], hid_up[1], by_above[0], by_above[1]):
            c.start()

    for i in range(4, 7):
        table_up[i].wait_recv()

    @pl.when(lo == 0)
    def _():
        table_last.wait_recv()
        table_3.wait_recv()

    @pl.when(lo == 1)
    def _():
        table_up[7].wait_recv()

    slope(hid, arr, 0, base_arr, s_arr, t_arr, GROUP)
    halve_own([(s_arr, arr, second)])

    @pl.when(lo == 1)
    def _():
        slope(oth, arr, 1, base_arr, s_oth, t_oth, GROUP)
        halve(1, [(s_oth, arr, second)], True)
        send_other()
        hid_up[2].start()
        leg_2_odd[0].wait_recv()
        leg_3_odd[0].start()

    @pl.when(lo == 0)
    def _():
        leg_1[1].wait_recv()
        leg_2[1].start()
        grad_up[0].wait_send()
        grad_up[3].start()
        table_term([(t_arr, hid)], GROUP, grad, F32)

    @pl.when(lo == 1)
    def _():
        table_term([(t_arr, hid), (t_oth, oth)], GROUP, grad, F32)

    send_rest()

    def finish(cut):
        grad[rows_of(cut)] = grad[rows_of(cut)] + dwr[rows_of(cut)].astype(F32)

    def finish_hidden():
        core_copy(0, hi).wait_recv()
        for h in range(2):
            for late in range(2):
                side_arrival(h, late).wait_recv()
        total = keep[hi] + cc_in[hi].astype(F32) + x_in[0].astype(F32) + x_in[1].astype(F32)
        gh_out[...] = total.astype(BF16)

    @pl.when(lo == 0)
    def _():
        count = len(GRAD_CUTS)
        leg_2[0].wait_recv()
        leg_3[0].start()
        for i in range(count):
            if i + 4 < count:
                grad_up[i + 1].wait_send()
                grad_up[i + 4].start()
            if i == 2:
                leg_2[1].wait_recv()
                leg_3[1].start()
            grad_up[i].wait_recv()
            finish(GRAD_CUTS[i])
        for i in range(2):
            leg_3[i].wait_recv()
            finish(LONG_CUTS[i])
        finish_hidden()
        for j, (h, low, size) in enumerate(SIDE_PARTS):
            by_back_in[j].wait_recv()
            finish((SIDE_CUTS[h][0] + low, size))
        for c in [table_1, table_2, table_3] + by_side + leg_1 + leg_2 + leg_3 + grad_up[count - 3:]:
            c.wait_send()

    def half_term(n):
        rows = pl.ds(n * 2 * quarter, 2 * quarter)

        def step(start):
            group = pl.ds(start, GROUP)
            value = slope_of(thr[rows, :], arr[group, :], 2, rows, base_arr, start)
            t_thr[n, group, :] = value.T.astype(BF16)

            def body(wide):
                grad[group, wide] += jnp.dot(t_thr[n, group, :], thr[rows, wide], preferred_element_type=F32)
            each_wide(body)
        each_group(step)

    @pl.when(lo == 1)
    def _():
        hid_up[3].start()
        leg_2_odd[1].wait_recv()
        leg_3_odd[1].start()
        for j in range(2):
            by_above[j].wait_recv()
            by_back[j].start()
        for c in hid_up[:3]:
            c.wait_recv()
        hid_relay[0].start()
        hid_relay[0].wait_recv()
        half_term(0)
        for i in range(2):
            leg_3_odd[i].wait_recv()
            hid_relay[2 + i].start()
        finish_hidden()
        hid_up[3].wait_recv()
        hid_relay[1].start()
        for c in hid_relay[1:]:
            c.wait_recv()
        half_term(1)
        for c in hid_up:
            c.wait_send()
        for c in leg_1_odd + leg_2_odd + leg_3_odd + hid_relay + by_back + by_above:
            c.wait_send()

    aux_side.wait_send()
    aux_up.wait_send()
    for c in hidden_out + relay:
        c.wait_send()
    for tok in range(2):
        for h in range(2):
            core_copy(tok, h).wait_send()
    for h in range(2):
        cross_arrival(h).wait_send()
        for late in range(2):
            side_arrival(h, late).wait_send()


def per_device(rows_of_ring, hidden, table, targets, group_start, log_norm, loss_grad):
    tokens, width = hidden.shape
    vocab = table.shape[0]
    quarter = tokens // 4
    padded = -(-tokens // 128) * 128
    dma = pltpu.SemaphoreType.DMA
    return pl.pallas_call(
        functools.partial(kernel, rows_of_ring),
        out_shape=(
            pltpu.VMEM((quarter, width), BF16),
            pltpu.VMEM((vocab, width), F32),
        ),
        in_specs=[
            pl.BlockSpec(memory_space=pltpu.VMEM),
            pl.BlockSpec(memory_space=pltpu.SMEM),
            pl.BlockSpec(memory_space=pltpu.VMEM),
            pl.BlockSpec(memory_space=pltpu.VMEM),
            pl.BlockSpec(memory_space=pl.ANY),
            pl.BlockSpec(memory_space=pl.ANY),
        ],
        out_specs=[pl.BlockSpec(memory_space=pltpu.VMEM)] * 2,
        scratch_shapes=[
            *[pltpu.VMEM((tokens, width), BF16)] * 3,
            *[pltpu.VMEM((vocab, width), BF16)] * 2,
            *[pltpu.VMEM((8, padded), F32)] * 3,
            pltpu.VMEM((3, tokens, 128), F32),
            *[pltpu.VMEM((tokens, vocab), BF16)] * 3,
            *[pltpu.VMEM((vocab, tokens), BF16)] * 3,
            pltpu.VMEM((2, vocab, tokens // 2), BF16),
            *[pltpu.VMEM((vocab, width), BF16)] * 2,
            *[pltpu.VMEM((4, quarter, width), F32)] * 2,
            *[pltpu.VMEM((4, quarter, width), BF16)] * 2,
            pltpu.VMEM((3, quarter, width), BF16),
            pltpu.VMEM((2, quarter, width), BF16),
            pltpu.VMEM((2, quarter, width // 2), BF16),
            *[pltpu.VMEM((LONG_ROWS, width), BF16)] * 2,
            *[pltpu.VMEM((2, SIDE_CUTS[0][1], width), BF16)] * 2,
            dma((2,)), dma((COPIES,)), dma((COPIES,)),
        ],
        compiler_params=pltpu.CompilerParams(
            collective_id=1, has_side_effects=True, vmem_limit_bytes=56 * 2**20
        ),
        cost_estimate=pl.CostEstimate(
            flops=18 * tokens * vocab * width, bytes_accessed=12 * tokens * width, transcendentals=3 * tokens * vocab
        ),
    )(targets, group_start, log_norm, loss_grad, hidden, table)


def solution(mesh):
    placed = (P("blk", None), P(("blk", "vocab"), None), P("blk"), P("blk"), P("blk"), P("blk"))
    return jax.shard_map(
        functools.partial(per_device, mesh.shape["blk"] // 2),
        mesh=mesh,
        in_specs=placed,
        out_specs=(P(("blk", "vocab"), None), P(("blk", "vocab"), None)),
        check_vma=False,
    )
```

```python
import functools

import jax
import jax.numpy as jnp
from jax import lax
from jax.experimental import pallas as pl
from jax.experimental.pallas import tpu as pltpu
from jax.sharding import PartitionSpec as P

MESH = pl.DeviceIdType.MESH
GROUP = 256
WIDE = 768
RING, LEG = 8, 3
TABLE_CUTS = tuple((64 * i, 64) for i in range(8))
GRAD_CUTS = tuple((64 * i, 64) for i in range(5)) + ((320, 48),)
SIDE_CUTS = ((368, 32), (400, 32))
LONG_CUTS = ((432, 48), (480, 32))
SIDE_PARTS = ((0, 0, 32), (1, 0, 32))
LONG_TABLE = (496, 16)
LONG_ROWS = 112
HID_CUTS = ((0, 0, 64), (0, 64, 64), (0, 128, 48), (1, 0, 64))
HID_LONG = ((1, 64, 64), (1, 128, 48))
HID_SHARE = ((0, 0, 176), (1, 0, 64)) + HID_LONG
F32, BF16 = jnp.float32, jnp.bfloat16

AUX, SIDE_HID, SIDE_RELAY, CORE, CROSS, SIDE = 0, 2, 4, 6, 10, 12
TABLE = 16
GRAD = TABLE + len(TABLE_CUTS)
LONG = GRAD + len(GRAD_CUTS)
HID_UP = LONG + 6
HID_RELAY = HID_UP + len(HID_CUTS)
BY_SIDE = HID_RELAY + len(HID_SHARE)
BY_UP = BY_SIDE + 2
BY_BACK = BY_UP + 2
LONG_TAB = BY_BACK + 2
COPIES = LONG_TAB + 3


def kernel(
    rows_of_ring, tgt_ref, first_ref, norm_ref, cot_ref, hid_hbm, tab_hbm, gh_out, grad,
    hid, oth, thr, tab, arr, aux_ref, aux_oth, aux_arr, cols,
    s_own, s_oth, s_arr, t_own, t_oth, t_arr, t_thr,
    dwp, dwr, keep, give, cc_out, cc_in, x_out, x_in, m_in, way_a, way_b, by_in, by_up, lsem, send, recv,
):
    tokens, width = hid.shape
    vocab = tab.shape[0]
    quarter = tokens // 4
    blk, part = lax.axis_index("blk"), lax.axis_index("vocab")
    row, lo = blk // 2, blk % 2
    hi, core = part // 2, part % 2
    plane, height = row // RING, row % RING

    def at(r, low, high, c):
        return (((r + rows_of_ring) % rows_of_ring) * 2 + low, high * 2 + c)

    def along(y, z):
        return y * RING + (z + RING) % RING

    up, down = at(row + 1, lo, hi, core), at(row - 1, lo, hi, core)
    side = [at(row, 1 - lo, h, core) for h in range(2)]
    sibling = at(row, lo, hi, 1 - core)
    turn_to = lax.rem(height + RING + LEG, RING) == RING - 1
    turn_from = lax.rem(height + 2 * LEG, RING) == RING - 1
    leg_to = at(along(plane, height - LEG), lo, hi, core)
    leg_from = at(along(plane, height + LEG), lo, hi, core)
    turn_to = at(along(plane + turn_to.astype(jnp.int32), height - LEG), lo, hi, core)
    turn_from = at(along(plane - turn_from.astype(jnp.int32), height + LEG), lo, hi, core)
    last_to = at(along(plane, height - 1), lo, hi, core)
    last_from = at(along(plane, height + 1), lo, hi, core)

    barrier = pltpu.get_barrier_semaphore()
    partners = (up, down, side[0], side[1], sibling, leg_to, leg_from, turn_to, turn_from, last_to, last_from)
    for device in partners:
        pl.semaphore_signal(barrier, inc=1, device_id=device, device_id_type=MESH)

    load_hid = pltpu.make_async_copy(hid_hbm, hid, lsem.at[0])
    load_tab = pltpu.make_async_copy(tab_hbm, tab, lsem.at[1])
    load_hid.start()
    load_tab.start()

    aux_ref[...] = jnp.zeros_like(aux_ref)
    aux_ref[0:1, :tokens] = tgt_ref[...].astype(F32).reshape(1, tokens)
    aux_ref[1:2, :tokens] = norm_ref[...].reshape(1, tokens)
    aux_ref[2:3, :tokens] = cot_ref[...].reshape(1, tokens)
    aux_ref[3:4, :] = jnp.full((1, aux_ref.shape[1]), first_ref[0].astype(F32), F32)

    pl.semaphore_wait(barrier, len(partners))

    def quarter_of(h, c):
        return pl.ds(pl.multiple_of((h * 2 + c) * quarter, 16), quarter)

    def rows_of(cut):
        return pl.ds(cut[0], cut[1])

    def copy(src, dst, number, device, number_there=None):
        there = number if number_there is None else number_there
        return pltpu.make_async_remote_copy(
            src_ref=src, dst_ref=dst, send_sem=send.at[number], recv_sem=recv.at[there],
            device_id=device, device_id_type=MESH,
        )

    table_up = [copy(tab_hbm.at[rows_of(c)], arr.at[rows_of(c)], TABLE + i, up) for i, c in enumerate(TABLE_CUTS)]
    grad_up = [copy(dwp.at[rows_of(c)], dwr.at[rows_of(c)], GRAD + i, up) for i, c in enumerate(GRAD_CUTS)]

    def piece_of(cut):
        return pl.ds(pl.multiple_of((cut[0] * 2 + core) * quarter + cut[1], 16), cut[2])

    def legs(sources, targets, sizes):
        first, second, third, place = [], [], [], 0
        for i, (source, target, size) in enumerate(zip(sources, targets, sizes)):
            stop = pl.ds(place, size)
            first.append(copy(source, way_a.at[stop], LONG + i, leg_to))
            second.append(copy(way_a.at[stop], way_b.at[stop], LONG + 2 + i, turn_to))
            third.append(copy(way_b.at[stop], target, LONG + 4 + i, last_to))
            place += size
        return first, second, third

    leg_1, leg_2, leg_3 = legs(
        [dwp.at[rows_of(c)] for c in LONG_CUTS], [dwr.at[rows_of(c)] for c in LONG_CUTS], [c[1] for c in LONG_CUTS]
    )
    leg_1_odd, leg_2_odd, leg_3_odd = legs(
        [hid_hbm.at[piece_of(h)] for h in HID_LONG], [thr.at[piece_of(h)] for h in HID_LONG], [h[2] for h in HID_LONG]
    )

    last = TABLE_CUTS[-1][0]
    rest = pl.ds(last, LONG_TABLE[0] - last)
    table_last = copy(tab_hbm.at[rest], arr.at[rest], TABLE + len(TABLE_CUTS) - 1, up)
    spare = pl.ds(LONG_ROWS - LONG_TABLE[1], LONG_TABLE[1])
    table_1 = copy(tab_hbm.at[rows_of(LONG_TABLE)], way_a.at[spare], LONG_TAB, leg_to)
    table_2 = copy(way_a.at[spare], way_b.at[spare], LONG_TAB + 1, turn_to)
    table_3 = copy(way_b.at[spare], arr.at[rows_of(LONG_TABLE)], LONG_TAB + 2, last_to)

    hid_up = [copy(hid_hbm.at[piece_of(h)], thr.at[piece_of(h)], HID_UP + i, up) for i, h in enumerate(HID_CUTS)]
    hid_relay = [copy(thr.at[piece_of(h)], thr.at[piece_of(h)], HID_RELAY + i, sibling) for i, h in enumerate(HID_SHARE)]

    by_side = [copy(dwp.at[rows_of(c)], by_in.at[hi], BY_SIDE + g, side[g], BY_SIDE + hi) for g, c in enumerate(SIDE_CUTS)]
    by_side_in = [copy(by_in.at[h], by_in.at[h], BY_SIDE + h, side[h]) for h in range(2)]
    by_above, by_back, by_back_in = [], [], []
    for j, (h, low, size) in enumerate(SIDE_PARTS):
        there = SIDE_CUTS[0][0] + low
        rows = pl.ds(low, size)
        back = pl.ds(pl.multiple_of(there + hi * SIDE_CUTS[0][1], 16), size)
        by_above.append(copy(by_in.at[h, rows], by_up.at[h, rows], BY_UP + j, up))
        by_back.append(copy(by_up.at[h, rows], dwr.at[back], BY_BACK + j, side[h], BY_BACK + 2 * (j // 2) + hi))
        landed = pl.ds(there + h * SIDE_CUTS[0][1], size)
        by_back_in.append(copy(by_up.at[h, rows], dwr.at[landed], BY_BACK + j, side[h]))

    mine = quarter_of(hi, core)
    hidden_out = [copy(hid_hbm.at[mine], oth.at[mine], SIDE_HID + h, side[h], SIDE_HID + hi) for h in range(2)]
    hidden_in = [copy(oth.at[quarter_of(h, core)], oth.at[quarter_of(h, core)], SIDE_HID + h, side[h]) for h in range(2)]
    relay = [copy(oth.at[quarter_of(h, core)], oth.at[quarter_of(h, core)], SIDE_RELAY + h, sibling) for h in range(2)]
    aux_side = copy(aux_ref, aux_oth, AUX, at(row, 1 - lo, hi, core))
    aux_up = copy(aux_ref, aux_arr, AUX + 1, up)

    aux_side.start()
    for c in hidden_out:
        c.start()
    aux_up.start()
    for i in range(3):
        table_up[i].start()

    @pl.when(lo == 0)
    def _():
        table_1.start()

    @pl.when(lo == 1)
    def _():
        for c in leg_1_odd:
            c.start()

    def spread(ref, slot):
        for i in range(ref.shape[1] // 128):
            block = ref[:, i * 128:(i + 1) * 128]
            square = jnp.concatenate([block] * 16, axis=0)
            rest = min(128, tokens - i * 128)
            cols[slot, i * 128:i * 128 + rest, :] = square.T[:rest]

    def slope_of(hid_rows, tab_rows, slot, rows, base, start):
        logits = lax.dot_general(
            hid_rows, tab_rows, (((1,), (1,)), ((), ())), preferred_element_type=F32
        )
        ids = (lax.broadcasted_iota(jnp.int32, (1, GROUP), 1) + (part * vocab + start)).astype(F32)
        hit = (cols[slot, rows, 0:1] == base + ids).astype(F32)
        return cols[slot, rows, 2:3] * (jnp.exp(logits - cols[slot, rows, 1:2]) - hit)

    def slope(hid_ref, tab_ref, slot, base, out, out_t, start):
        group = pl.ds(start, GROUP)
        value = slope_of(hid_ref[...], tab_ref[group, :], slot, pl.ds(0, tokens), base, start)
        out[:, group] = value.astype(BF16)
        out_t[group, :] = value.T.astype(BF16)

    def each_group(body):
        def step(i, carry):
            body(pl.multiple_of(i * GROUP, GROUP))
            return carry
        lax.fori_loop(0, vocab // GROUP, step, 0)

    def each_wide(body):
        def step(i, carry):
            body(pl.ds(pl.multiple_of(i * WIDE, WIDE), WIDE))
            return carry
        lax.fori_loop(0, width // WIDE, step, 0)

    def table_term(terms, start, out, dtype):
        group = pl.ds(start, GROUP)

        def body(wide):
            total = None
            for st, h in terms:
                term = jnp.dot(st[group, :], h[:, wide], preferred_element_type=F32)
                total = term if total is None else total + term
            out[group, wide] = total.astype(dtype)
        each_wide(body)

    def hidden_term(terms, rows, store):
        def body(wide):
            total = None
            for s, t, span in terms:
                term = jnp.dot(s[rows, span], t[span, wide], preferred_element_type=F32)
                total = term if total is None else total + term
            store(wide, total)
        each_wide(body)

    def core_copy(tok, h):
        slot = tok * 2 + h
        return copy(cc_out.at[slot], cc_in.at[slot], CORE + slot, sibling)

    def begin(tok, terms):
        for h in range(2):
            for c, place in ((1 - core, give), (core, keep)):
                def put(wide, value, place=place, slot=tok * 2 + h):
                    place[slot, :, wide] = value
                hidden_term(terms, quarter_of(h, c), put)

    def halve(tok, terms, begun):
        for h in range(2):
            def put(wide, value, slot=tok * 2 + h):
                if begun:
                    value = value + give[slot, :, wide]
                cc_out[slot, :, wide] = value.astype(BF16)
            hidden_term(terms, quarter_of(h, 1 - core), put)
            core_copy(tok, h).start()
        for h in range(2):
            def put(wide, value, slot=tok * 2 + h):
                if begun:
                    value = value + keep[slot, :, wide]
                keep[slot, :, wide] = value
            hidden_term(terms, quarter_of(h, core), put)

    half = width // 2

    def columns(g):
        return pl.ds(pl.multiple_of(g * half, 128), half)

    def cross_copy(g):
        return copy(x_out.at[0, :, columns(g)], m_in.at[hi], CROSS + g, side[g], CROSS + hi)

    def cross_arrival(g):
        return copy(x_out.at[0, :, columns(g)], m_in.at[g], CROSS + g, side[g])

    def side_copy(h, late):
        span = columns(hi if late else 1 - hi)
        return copy(
            x_out.at[1 + h, :, span], x_in.at[hi, :, span], SIDE + 2 * h + late, side[h], SIDE + 2 * hi + late
        )

    def side_arrival(h, late):
        span = columns(h if late else 1 - h)
        return copy(x_out.at[1 + h, :, span], x_in.at[h, :, span], SIDE + 2 * h + late, side[h])

    def halve_own(terms):
        def share(h):
            def put(wide, value):
                cc_out[h, :, wide] = (value + give[h, :, wide]).astype(BF16)
            hidden_term(terms, quarter_of(h, 1 - core), put)
            core_copy(0, h).start()

        def hold(h):
            def put(wide, value):
                keep[h, :, wide] = value + keep[h, :, wide]
            hidden_term(terms, quarter_of(h, core), put)

        share(1 - hi)
        hold(1 - hi)
        share(hi)
        core_copy(0, 1 - hi).wait_recv()
        x_out[0] = (keep[1 - hi] + cc_in[1 - hi].astype(F32)).astype(BF16)
        for g in range(2):
            cross_copy(g).start()
        hold(hi)

    def send_other():
        for h in range(2):
            core_copy(1, h).wait_recv()
            span = columns(1 - hi)
            x_out[1 + h, :, span] = (keep[2 + h, :, span] + cc_in[2 + h, :, span].astype(F32)).astype(BF16)
            side_copy(h, 0).start()

    def send_rest():
        for h in range(2):
            cross_arrival(1 - h).wait_recv()
            span = columns(hi)
            value = keep[2 + h, :, span] + cc_in[2 + h, :, span].astype(F32) + m_in[1 - h].astype(F32)
            x_out[1 + h, :, span] = value.astype(BF16)
            side_copy(h, 1).start()

    whole, first, second = pl.ds(0, vocab), pl.ds(0, GROUP), pl.ds(GROUP, GROUP)

    spread(aux_ref, 0)
    load_hid.wait()
    load_tab.wait()
    base_own = aux_ref[3:4, 0:1]
    each_group(lambda start: slope(hid, tab, 0, base_own, s_own, t_own, start))

    table_up[0].wait_send()
    table_up[3].start()
    for h in range(2):
        hidden_in[h].wait_recv()
        relay[h].start()
    aux_side.wait_recv()
    spread(aux_oth, 1)
    for h in range(2):
        relay[h].wait_recv()
    for i in range(1, 3):
        table_up[i].wait_send()
        table_up[i + 3].start()

    @pl.when(lo == 0)
    def _():
        table_1.wait_recv()
        table_2.start()
        each_group(lambda start: slope(oth, tab, 1, base_own, s_oth, t_oth, start))
        table_term([(t_own, hid), (t_oth, oth)], GROUP, dwp, BF16)
        table_2.wait_recv()
        table_3.start()
        for c in by_side + leg_1:
            c.start()
        halve(1, [(s_oth, tab, whole)], False)
        send_other()
        table_term([(t_own, hid), (t_oth, oth)], 0, dwp, BF16)

    @pl.when(lo == 1)
    def _():
        leg_1_odd[0].wait_recv()
        leg_2_odd[0].start()

    table_up[3].wait_send()
    table_up[6].start()
    table_up[4].wait_send()

    @pl.when(lo == 0)
    def _():
        table_last.start()

    @pl.when(lo == 1)
    def _():
        table_up[7].start()


    @pl.when(lo == 1)
    def _():
        leg_1_odd[1].wait_recv()
        leg_2_odd[1].start()

    aux_up.wait_recv()
    base_arr = aux_arr[3:4, 0:1]
    for i in range(4):
        table_up[i].wait_recv()
    slope(hid, arr, 0, base_arr, s_arr, t_arr, 0)

    @pl.when(lo == 0)
    def _():
        begin(0, [(s_own, tab, whole), (s_arr, arr, first)])
        table_term([(t_arr, hid)], 0, grad, F32)

    @pl.when(lo == 1)
    def _():
        slope(oth, arr, 1, base_arr, s_oth, t_oth, 0)
        begin(1, [(s_oth, arr, first)])
        begin(0, [(s_own, tab, whole), (s_arr, arr, first)])
        table_term([(t_arr, hid), (t_oth, oth)], 0, grad, F32)

    @pl.when(lo == 0)
    def _():
        leg_1[0].wait_recv()
        leg_2[0].start()
        for i in range(5, 7):
            table_up[i].wait_send()
        table_last.wait_send()
        for i in range(3):
            grad_up[i].start()

    @pl.when(lo == 1)
    def _():
        spread(aux_arr, 2)
        for i in range(5, 8):
            table_up[i].wait_send()
        for c in by_side_in:
            c.wait_recv()
        for c in (hid_up[0], hid_up[1], by_above[0], by_above[1]):
            c.start()

    for i in range(4, 7):
        table_up[i].wait_recv()

    @pl.when(lo == 0)
    def _():
        table_last.wait_recv()
        table_3.wait_recv()

    @pl.when(lo == 1)
    def _():
        table_up[7].wait_recv()

    slope(hid, arr, 0, base_arr, s_arr, t_arr, GROUP)
    halve_own([(s_arr, arr, second)])

    @pl.when(lo == 1)
    def _():
        slope(oth, arr, 1, base_arr, s_oth, t_oth, GROUP)
        halve(1, [(s_oth, arr, second)], True)
        send_other()
        hid_up[2].start()
        hid_up[3].start()
        leg_2_odd[0].wait_recv()
        leg_3_odd[0].start()

    @pl.when(lo == 0)
    def _():
        leg_1[1].wait_recv()
        leg_2[1].start()
        grad_up[0].wait_send()
        grad_up[3].start()
        table_term([(t_arr, hid)], GROUP, grad, F32)

    @pl.when(lo == 1)
    def _():
        table_term([(t_arr, hid), (t_oth, oth)], GROUP, grad, F32)

    send_rest()

    def finish(cut):
        grad[rows_of(cut)] = grad[rows_of(cut)] + dwr[rows_of(cut)].astype(F32)

    def finish_hidden():
        core_copy(0, hi).wait_recv()
        for h in range(2):
            for late in range(2):
                side_arrival(h, late).wait_recv()
        total = keep[hi] + cc_in[hi].astype(F32) + x_in[0].astype(F32) + x_in[1].astype(F32)
        gh_out[...] = total.astype(BF16)

    @pl.when(lo == 0)
    def _():
        count = len(GRAD_CUTS)
        leg_2[0].wait_recv()
        leg_3[0].start()
        for i in range(count):
            if i + 4 < count:
                grad_up[i + 1].wait_send()
                grad_up[i + 4].start()
            if i == 2:
                leg_2[1].wait_recv()
                leg_3[1].start()
            if i == count - 1:
                for n in range(2):
                    leg_3[n].wait_recv()
                    finish(LONG_CUTS[n])
                finish_hidden()
            grad_up[i].wait_recv()
            finish(GRAD_CUTS[i])
        for j, (h, low, size) in enumerate(SIDE_PARTS):
            by_back_in[j].wait_recv()
            finish((SIDE_CUTS[h][0] + low, size))
        for c in [table_1, table_2, table_3] + by_side + leg_1 + leg_2 + leg_3 + grad_up[count - 3:]:
            c.wait_send()

    def half_term(n):
        rows = pl.ds(n * 2 * quarter, 2 * quarter)

        def step(start):
            group = pl.ds(start, GROUP)
            value = slope_of(thr[rows, :], arr[group, :], 2, rows, base_arr, start)
            t_thr[n, group, :] = value.T.astype(BF16)

            def body(wide):
                grad[group, wide] += jnp.dot(t_thr[n, group, :], thr[rows, wide], preferred_element_type=F32)
            each_wide(body)
        each_group(step)

    @pl.when(lo == 1)
    def _():
        leg_2_odd[1].wait_recv()
        leg_3_odd[1].start()
        for j in range(2):
            by_above[j].wait_recv()
            by_back[j].start()
        for c in hid_up[:3]:
            c.wait_recv()
        hid_relay[0].start()
        hid_relay[0].wait_recv()
        half_term(0)
        for i in range(2):
            leg_3_odd[i].wait_recv()
            hid_relay[2 + i].start()
        finish_hidden()
        hid_up[3].wait_recv()
        hid_relay[1].start()
        for c in hid_relay[1:]:
            c.wait_recv()
        half_term(1)
        for c in hid_up:
            c.wait_send()
        for c in leg_1_odd + leg_2_odd + leg_3_odd + hid_relay + by_back + by_above:
            c.wait_send()

    aux_side.wait_send()
    aux_up.wait_send()
    for c in hidden_out + relay:
        c.wait_send()
    for tok in range(2):
        for h in range(2):
            core_copy(tok, h).wait_send()
    for h in range(2):
        cross_arrival(h).wait_send()
        for late in range(2):
            side_arrival(h, late).wait_send()


def per_device(rows_of_ring, hidden, table, targets, group_start, log_norm, loss_grad):
    tokens, width = hidden.shape
    vocab = table.shape[0]
    quarter = tokens // 4
    padded = -(-tokens // 128) * 128
    dma = pltpu.SemaphoreType.DMA
    return pl.pallas_call(
        functools.partial(kernel, rows_of_ring),
        out_shape=(
            pltpu.VMEM((quarter, width), BF16),
            pltpu.VMEM((vocab, width), F32),
        ),
        in_specs=[
            pl.BlockSpec(memory_space=pltpu.VMEM),
            pl.BlockSpec(memory_space=pltpu.SMEM),
            pl.BlockSpec(memory_space=pltpu.VMEM),
            pl.BlockSpec(memory_space=pltpu.VMEM),
            pl.BlockSpec(memory_space=pl.ANY),
            pl.BlockSpec(memory_space=pl.ANY),
        ],
        out_specs=[pl.BlockSpec(memory_space=pltpu.VMEM)] * 2,
        scratch_shapes=[
            *[pltpu.VMEM((tokens, width), BF16)] * 3,
            *[pltpu.VMEM((vocab, width), BF16)] * 2,
            *[pltpu.VMEM((8, padded), F32)] * 3,
            pltpu.VMEM((3, tokens, 128), F32),
            *[pltpu.VMEM((tokens, vocab), BF16)] * 3,
            *[pltpu.VMEM((vocab, tokens), BF16)] * 3,
            pltpu.VMEM((2, vocab, tokens // 2), BF16),
            *[pltpu.VMEM((vocab, width), BF16)] * 2,
            *[pltpu.VMEM((4, quarter, width), F32)] * 2,
            *[pltpu.VMEM((4, quarter, width), BF16)] * 2,
            pltpu.VMEM((3, quarter, width), BF16),
            pltpu.VMEM((2, quarter, width), BF16),
            pltpu.VMEM((2, quarter, width // 2), BF16),
            *[pltpu.VMEM((LONG_ROWS, width), BF16)] * 2,
            *[pltpu.VMEM((2, SIDE_CUTS[0][1], width), BF16)] * 2,
            dma((2,)), dma((COPIES,)), dma((COPIES,)),
        ],
        compiler_params=pltpu.CompilerParams(
            collective_id=1, has_side_effects=True, vmem_limit_bytes=56 * 2**20
        ),
        cost_estimate=pl.CostEstimate(
            flops=18 * tokens * vocab * width, bytes_accessed=12 * tokens * width, transcendentals=3 * tokens * vocab
        ),
    )(targets, group_start, log_norm, loss_grad, hidden, table)


def solution(mesh):
    placed = (P("blk", None), P(("blk", "vocab"), None), P("blk"), P("blk"), P("blk"), P("blk"))
    return jax.shard_map(
        functools.partial(per_device, mesh.shape["blk"] // 2),
        mesh=mesh,
        in_specs=placed,
        out_specs=(P(("blk", "vocab"), None), P(("blk", "vocab"), None)),
        check_vma=False,
    )
```
